128 devices in a mesh: gz: 4 (over z), xy: 32 (over x, y, core).
Axes of the slice: x: 4, y: 4, z: 4, core: 2. Of those that a mesh axis runs over, the one named last changes fastest.
Arguments:
- areas: bfloat16 [262144, 512], P(('gz', 'xy')), may hold values from 0 to 1
- angles: float32 [2, 262144], P(None, ('gz', 'xy')), may hold values from -3.140625 to 3.140625
- transm: float32 [262144], P(('gz', 'xy')), may hold values from 0.1 to 1
- owner: int32 [262144, 1], P(('gz', 'xy')), may hold values from 0 to 127; in each aligned block of 2048 rows (0 to 2047, 2048 to 4095, ...) at most 24 rows name the same one
- tile: int32 [262144], P(('gz', 'xy')), may hold values from 0 to 511
- live_count: int32 [128], P(('gz', 'xy')), may hold values from 1024 to 2048, as said below
- rock: float32 [32, 512, 2048], P('gz', 'xy'), may hold values from 0.5 to 2
- source: float32 [32, 512, 2048], P('gz', 'xy'), may hold values from -6 to 6
- start: float32 [32, 512, 2048], P('gz', 'xy'), may hold values from -6 to 6
Outputs:
- perm: float32 [6, 32, 512, 2048], P(None, 'gz', 'xy')
- pressure: float32 [32, 512, 2048], P('gz', 'xy')
The draws below stay inside these ranges and needn't reach their ends.
Inputs may be any that keep to these rules, and one draw needn't show every extreme that they name: Within the rows of one device no owner is named more than 24 times, a bound that some block reaches. `live_count`: some device has exactly 2048 live rows.
All inputs are finite; a program needn't handle non-finite values.
Results may differ from the reference program's by a relative error of at most 0.0015.
Values may be sent and summed in bfloat16 or wider, within the bound.
A program may use at most 192 MiB of HBM per device.

```python
import functools
import math
import jax
import jax.numpy as jnp
import numpy as np
from jax import lax

CZ = 8
CY = 16
NX = 2048
E_DEV = 2048
TILE = 8
SWEEPS = 2
OWNERS = 128
E_ALL = 262144
CAP = 24
NZ = 32
NY = 512
TILES_DEV = 512
N_XY = 32


def draw_live_count(key, part):
    first_key = jax.random.fold_in(key, 11)
    second_key = jax.random.fold_in(key, 12)
    counts = jax.random.randint(first_key, (OWNERS,), E_DEV // 2, E_DEV + 1)
    chosen = jax.random.randint(second_key, (), 0, OWNERS)
    return counts.at[chosen].set(E_DEV).astype(jnp.int32)


def with_ends(array, own_key, low, largest):
    longest = array.shape.index(max(array.shape))
    spots = []
    for shift in (0, 1):
        where = [jax.random.randint(jax.random.fold_in(own_key, axis), (), 0, length) for axis, length in enumerate(array.shape)]
        where[longest] = (where[longest] + shift) % array.shape[longest]
        spots.append(tuple(where))
    return array.at[spots[0]].set(low).at[spots[1]].set(largest)


def level_of(own_key, extent, split, low, largest):
    def one(dim, blocks):
        draws = jax.random.uniform(jax.random.fold_in(jax.random.fold_in(own_key, 6), dim), (blocks,), jnp.float32, low / len(split), largest / len(split))
        return jnp.repeat(jnp.exp(draws), extent[dim] // blocks).reshape((-1,) + (1,) * (len(extent) - dim - 1))

    gain = one(*split[0])
    for cut in split[1:]:
        gain = gain * one(*cut)
    return gain


def deal_out(stream_key, own, number, rows, count, top, limit, skew):
    sequence = jax.random.permutation(stream_key, count)
    packed, common = portions_of(count, rows * top, limit, skew, True), portions_of(count, rows * top, limit, skew, False)
    places = jnp.arange(count)

    def named(sizes, rotation):
        used = int((sizes > 0).sum())
        fixed = max(1, used // 4)
        moved = fixed + (places - fixed + rotation * (used - fixed)) % max(1, count - fixed)
        return jnp.zeros((count,), jnp.int32).at[sequence[jnp.where(places < fixed, places, moved)]].set(jnp.asarray(sizes, jnp.int32))

    sizes = jnp.where(number % 4 == 0, named(packed, number // 4), named(common, number - number // 4 - 1))
    mixed = jax.random.permutation(jax.random.fold_in(own, 3), count)
    giver, receiver = mixed[0:count // 2 * 2:2], mixed[1:count // 2 * 2:2]
    room = jnp.minimum(sizes[giver] - 1, limit - sizes[receiver]) // 2
    room = jnp.where((giver == sequence[0]) | (receiver == sequence[0]) | (sizes[receiver] == 0), 0, jnp.maximum(room, 0))
    moved = jax.random.randint(jax.random.fold_in(own, 4), (count // 2,), 0, 1 << 20) % (room + 1)
    sizes = sizes.at[giver].add(-moved).at[receiver].add(moved)
    labels = jnp.searchsorted(jnp.cumsum(sizes), jnp.arange(rows * top), side="right").astype(jnp.int32)
    listing = labels.reshape(top, rows).T
    listing = listing[jax.random.permutation(jax.random.fold_in(own, 1), rows)]
    rotation = jax.random.randint(jax.random.fold_in(own, 2), (rows, 1), 0, top)
    return jnp.take_along_axis(listing, (jnp.arange(top)[None, :] + rotation) % top, axis=1)


def portions_of(number_of, total, bound, skew, full):
    weights = [(1 << 20) // math.isqrt(grade ** skew) + 1 for grade in range(1, number_of + 1)]
    largest = bound if full else min(bound, max(-(-total // number_of), total * weights[0] // sum(weights)))
    least = 1 if total - largest >= number_of - 1 else 0
    holding, spare = [largest] + [least] * (number_of - 1), total - largest - least * (number_of - 1)
    while spare > 0:
        candidates = [i for i in range(1, number_of) if holding[i] < largest] or [i for i in range(1, number_of) if holding[i] < bound]
        whole, budget = sum([weights[i] for i in candidates]), spare
        for i in candidates:
            more = min(bound - holding[i], max(1, budget * weights[i] // whole), spare)
            holding[i] = holding[i] + more
            spare = spare - more
    return np.array(holding)


def gaussian(key, shape, deviation, reach, cuts=(), kind=jnp.bfloat16):
    loudness = level_of(key, shape, cuts, -0.22, 0.18) if cuts else 1.0
    values = jax.random.normal(key, shape, jnp.float32) * deviation * loudness
    return jnp.minimum(jnp.maximum(values, -reach), reach).astype(kind)


def setup_inputs(seed: int = 0) -> dict:
    keys = jax.random.split(jax.random.key(seed), 10)
    areas = jnp.clip(1.0 * jax.random.uniform(keys[0], (E_ALL, TILE * TILE * TILE), jnp.float32) ** level_of(keys[0], (E_ALL, TILE * TILE * TILE), ((0, 128),), -0.2, 0.2), 0.0, 1.0).astype(jnp.bfloat16)
    angles = jnp.clip(jax.random.uniform(keys[1], (2, E_ALL), jnp.float32, -3.140625, 3.140625), -3.140625, 3.140625)
    transm = jnp.clip(jnp.exp(math.log(1.0) - 2.3025851 * jax.random.uniform(keys[2], (E_ALL,), jnp.float32) ** level_of(keys[2], (E_ALL,), ((0, 128),), -0.2, 0.2)), 0.1, 1.0)
    owner_keys = jax.random.split(jax.random.fold_in(keys[3], 1), E_ALL // E_DEV)
    owner_turns = jax.random.permutation(jax.random.fold_in(keys[3], 3), E_ALL // E_DEV)
    owner = jax.vmap(lambda own, number: deal_out(jax.random.fold_in(keys[3], 2), own, number, E_DEV, OWNERS, 1, CAP, 1))(owner_keys, owner_turns).reshape((E_ALL, 1))
    tile = with_ends(jax.random.randint(keys[4], (E_ALL,), 0, TILES_DEV), jax.random.fold_in(keys[4], 1), 0, TILES_DEV - 1).astype(jnp.int32)
    live_count = draw_live_count(jax.random.fold_in(keys[9], 71), 0)
    rock = jnp.clip(jnp.exp(math.log(2.0) - 1.3862944 * jax.random.uniform(keys[6], (NZ, NY, NX), jnp.float32) ** level_of(keys[6], (NZ, NY, NX), ((0, 4), (1, 32)), -0.2, 0.2)), 0.5, 2.0)
    source = gaussian(keys[7], (NZ, NY, NX), 1.0, 6.0, ((0, 4), (1, 32)), jnp.float32)
    start = gaussian(keys[8], (NZ, NY, NX), 1.0, 6.0, ((0, 4), (1, 32)), jnp.float32)
    return dict(areas=areas, angles=angles, transm=transm, owner=owner, tile=tile, live_count=live_count, rock=rock, source=source, start=start)


STEP_WEIGHTS = (1.0 / (1.0 - 0.7 * math.cos(math.pi / 4)), 1.0 / (1.0 + 0.7 * math.cos(math.pi / 4)))
FACE_OFFSETS = ((0, 0, 1), (0, 1, 0), (1, 0, 0))
CROSS_PAIRS = ((0, 1), (0, 2), (1, 2))


def tensor_parts(angles, transm):
    polar_sin = jnp.sin(angles[0])
    normal_x = polar_sin * jnp.cos(angles[1])
    normal_y = polar_sin * jnp.sin(angles[1])
    normal_z = jnp.cos(angles[0])
    parts = [transm * (1.0 - normal_x * normal_x), transm * (1.0 - normal_y * normal_y),
             transm * (1.0 - normal_z * normal_z), -transm * normal_x * normal_y,
             -transm * normal_x * normal_z, -transm * normal_y * normal_z]
    return jnp.stack(parts).astype(jnp.bfloat16)


def shifted(padded, step_z, step_y, step_x):
    return padded[1 + step_z:padded.shape[0] - 1 + step_z, 1 + step_y:padded.shape[1] - 1 + step_y,
                  1 + step_x:padded.shape[2] - 1 + step_x]


def coefficients(padded_coef):
    wider = jnp.pad(padded_coef, ((0, 0), (0, 0), (0, 0), (1, 1)))
    pieces = []
    for component in range(3):
        offset = FACE_OFFSETS[component]
        centre = shifted(wider[component], 0, 0, 0)
        forward = shifted(wider[component], offset[0], offset[1], offset[2])
        backward = shifted(wider[component], -offset[0], -offset[1], -offset[2])
        pieces.append(0.5 * (centre + forward))
        pieces.append(0.5 * (centre + backward))
    diagonal = functools.reduce(lambda left, right: left + right, pieces)
    cross = [0.25 * shifted(wider[3 + number], 0, 0, 0) for number in range(3)]
    return jnp.stack(pieces + cross), diagonal


def operate(padded_field, coef, diagonal):
    wider = jnp.pad(padded_field, ((0, 0), (0, 0), (1, 1)))
    total = diagonal * shifted(wider, 0, 0, 0)
    for position in range(3):
        offset = FACE_OFFSETS[position]
        total = total - coef[2 * position] * shifted(wider, offset[0], offset[1], offset[2])
        total = total - coef[2 * position + 1] * shifted(wider, -offset[0], -offset[1], -offset[2])
    for number in range(3):
        first = FACE_OFFSETS[CROSS_PAIRS[number][0]]
        second = FACE_OFFSETS[CROSS_PAIRS[number][1]]
        both_up = shifted(wider, first[0] + second[0], first[1] + second[1], first[2] + second[2])
        up_down = shifted(wider, first[0] - second[0], first[1] - second[1], first[2] - second[2])
        down_up = shifted(wider, second[0] - first[0], second[1] - first[1], second[2] - first[2])
        both_down = shifted(wider, -first[0] - second[0], -first[1] - second[1], -first[2] - second[2])
        total = total - coef[6 + number] * (both_up - up_down - down_up + both_down)
    return total


def reference(areas, angles, transm, owner, tile, live_count, rock, source, start):
    tensor = tensor_parts(angles, transm)
    row_index = jnp.arange(E_ALL, dtype=jnp.int32)
    device_of = row_index // E_DEV
    local_row = row_index % E_DEV
    live = local_row < live_count[device_of]
    kept = jnp.where(live[:, None], areas, jnp.zeros((), jnp.bfloat16))
    target = owner[:, 0]
    gz_of = target // N_XY
    xy_of = target % N_XY
    tz_count = CZ // TILE
    ty_count = CY // TILE
    tx_count = NX // TILE
    tz_local = tile // (ty_count * tx_count)
    ty_local = (tile // tx_count) % ty_count
    tx_local = tile % tx_count
    global_tile = ((gz_of * tz_count + tz_local) * (NY // TILE) + xy_of * ty_count + ty_local) * tx_count + tx_local
    total_tiles = (NZ // TILE) * (NY // TILE) * tx_count
    cells = TILE * TILE * TILE
    blocks = (kept.reshape(OWNERS, E_DEV, cells), jnp.transpose(tensor).reshape(OWNERS, E_DEV, 6),
              global_tile.reshape(OWNERS, E_DEV))

    def accumulate(carry, block):
        block_area, block_tensor, block_tile = block
        contrib = block_tensor.astype(jnp.float32)[:, :, None] * block_area.astype(jnp.float32)[:, None, :]
        return carry.at[block_tile].add(contrib), None

    summed, unused = lax.scan(accumulate, jnp.zeros((total_tiles, 6, cells), jnp.float32), blocks)
    summed = summed.reshape(NZ // TILE, NY // TILE, tx_count, 6, TILE, TILE, TILE)
    fracture = jnp.transpose(summed, (3, 0, 4, 1, 5, 2, 6)).reshape(6, NZ, NY, NX)
    perm = jnp.concatenate([fracture[:3] + rock[None], fracture[3:]], 0)
    coef, diagonal = coefficients(jnp.pad(perm, ((0, 0), (1, 1), (1, 1), (0, 0))))
    field = start
    for sweep_num in range(SWEEPS):
        for weight in STEP_WEIGHTS:
            padded_field = jnp.pad(field, ((1, 1), (1, 1), (0, 0)))
            field = field + weight * (source - operate(padded_field, coef, diagonal)) / diagonal
    return perm, field
```

```python
import functools
import math

import jax
import jax.numpy as jnp
import numpy as np
from jax import lax
from jax.experimental import pallas as pl
from jax.experimental.pallas import tpu as pltpu
from jax.sharding import PartitionSpec as P

TILE = 8
SWEEPS = 2
CAP = 24
CELLS = TILE * TILE * TILE
LANES = 128
STEP_WEIGHTS = (
    1.0 / (1.0 - 0.7 * math.cos(math.pi / 4)),
    1.0 / (1.0 + 0.7 * math.cos(math.pi / 4)),
)
MESH = pl.DeviceIdType.MESH
F32 = jnp.float32
BF16 = jnp.bfloat16


def grid_of(mesh):
    gz, xy = mesh.shape["gz"], mesh.shape["xy"]
    return (gz, 4, 4, 2) if xy == 32 else (gz, xy // 2, 1, 2)


def offset_of(step, dims):
    nz, nx, ny, nc = dims
    core = step % nc
    rest = step // nc
    a, b, c = rest % nz, (rest // nz) % nx, rest // (nz * nx)
    return a, (3 * a + b) % nx, (a + 2 * b + c) % ny, core


def step_of(dz, dx, dy, dc, dims):
    nz, nx, ny, nc = dims
    b = (dx - 3 * dz) % nx
    c = (dy - dz - 2 * b) % ny
    return ((c * nx + b) * nz + dz) * nc + dc


def place(dims):
    nz, nx, ny, nc = dims
    gz, xy = lax.axis_index("gz"), lax.axis_index("xy")
    return gz, xy // (ny * nc), (xy // nc) % ny, xy % nc


def moved(me, by, dims):
    z, x, y, c = [(m + d) % n for m, d, n in zip(me, by, dims)]
    return z, (x * dims[2] + y) * dims[3] + c


def permutations(dims):
    nz, nx, ny, nc = dims
    total = nz * nx * ny * nc
    groups, others = nz * nc, nx * ny
    first = np.zeros((total, total), np.float32)
    second = np.zeros((total, total), np.float32)
    third = np.zeros((total, total), np.float32)
    for step in range(total):
        dz, dx, dy, dc = offset_of(step, dims)
        u, w = dz * nc + dc, dx * ny + dy
        first[u * others + w, step] = 1
        second[w * groups + u, u * others + w] = 1
        third[w * groups + u, step] = 1
    return [jnp.asarray(m, BF16) for m in (first, second, third)]


def tensor_rows(angles, transm):
    polar_sin = jnp.sin(angles[0])
    normal_x = polar_sin * jnp.cos(angles[1])
    normal_y = polar_sin * jnp.sin(angles[1])
    normal_z = jnp.cos(angles[0])
    parts = [
        transm * (1.0 - normal_x * normal_x),
        transm * (1.0 - normal_y * normal_y),
        transm * (1.0 - normal_z * normal_z),
        -transm * normal_x * normal_y,
        -transm * normal_x * normal_z,
        -transm * normal_y * normal_z,
    ]
    return jnp.stack(parts).astype(BF16).astype(F32)


def dot(a, b):
    return jnp.dot(a, b, preferred_element_type=F32)


def iota(shape, dim):
    return lax.broadcasted_iota(jnp.int32, shape, dim)


def gather_kernel(
    dims,
    step_ref,
    meta_ref,
    areas_ref,
    first_ref,
    second_ref,
    third_ref,
    acc_ref,
    slot_ref,
    picked_ref,
    send_ref,
    recv_ref,
    near_out,
    near_in,
    far_out,
    far_in,
    turned_ref,
    column_ref,
    cell_ref,
    flip_ref,
    send_sem,
    recv_sem,
    near_send,
    near_recv,
    far_send,
    far_recv,
):
    nz, nx, ny, nc = dims
    total = nz * nx * ny * nc
    groups, others = nz * nc, nx * ny
    rows = areas_ref.shape[0]
    me = place(dims)
    send_chunk = total // 8
    recv_chunk = total // 4
    depth = recv_chunk * CAP

    barrier = pltpu.get_barrier_semaphore()

    def greet(step, carry):
        to = moved(me, offset_of(step, dims), dims)
        pl.semaphore_signal(barrier, inc=1, device_id=to, device_id_type=MESH)
        return carry

    lax.fori_loop(1, total, greet, 0)

    step_row = step_ref[...]
    marks = (step_row == iota((total, rows), 0)).astype(F32)
    width = min(rows, 256)
    upper = (iota((width, width), 0) <= iota((width, width), 1)).astype(BF16)
    carry = jnp.zeros((total, 1), F32)
    ranks = []
    for block in range(rows // width):
        part = marks[:, block * width : (block + 1) * width]
        running = dot(part.astype(BF16), upper) + carry
        carry = running[:, width - 1 : width]
        ranks.append(jnp.sum(running * part, axis=0, keepdims=True) - 1.0)
    rank = jnp.concatenate(ranks, axis=1)
    step_float = step_row.astype(F32)
    slot_ref[...] = jnp.where(step_float >= 0, step_float * CAP + rank, -1.0)

    chosen = (rank == iota((32, rows), 0).astype(F32)).astype(F32)
    spread = jnp.concatenate([chosen * meta_ref[v : v + 1, :] for v in range(8)], axis=0)
    sheet = lax.dot_general(
        marks.astype(BF16), spread.astype(BF16), (((1,), (1,)), ((), ())), preferred_element_type=F32
    )
    sheet = dot(first_ref[...], sheet.astype(BF16))
    near_out[...] = sheet.reshape(near_out.shape)

    pl.semaphore_wait(barrier, total - 1)

    def near_copy(u):
        return pltpu.make_async_remote_copy(
            near_out.at[u],
            near_in.at[u],
            near_send,
            near_recv,
            device_id=moved(me, (u // nc, 0, 0, u % nc), dims),
            device_id_type=MESH,
        )

    def far_copy(w):
        return pltpu.make_async_remote_copy(
            far_out.at[w],
            far_in.at[w],
            far_send,
            far_recv,
            device_id=moved(me, (0, w // ny, w % ny, 0), dims),
            device_id_type=MESH,
        )

    def start_all(copy):
        def one(index, carry):
            copy(index).start()
            return carry

        return one

    def drain(ref, first, count, sem):
        part = ref.at[pl.ds(first, count)]
        pltpu.make_async_copy(part, part, sem).wait()

    lax.fori_loop(1, groups, start_all(near_copy), 0)
    near_in[0] = near_out[0]

    def send_part(chunk, carry):
        base = chunk * send_chunk
        wanted = (iota((send_chunk * CAP, rows), 0) + base * CAP).astype(F32)
        pick = (slot_ref[...] == wanted).astype(F32).astype(BF16)
        picked_ref[...] = dot(pick, areas_ref[...])

        def one(index, carry):
            step = base + index
            block = picked_ref[pl.ds(pl.multiple_of(index * CAP, 8), CAP), :]
            parts = [block[:, c * LANES : (c + 1) * LANES] for c in range(CELLS // LANES)]
            send_ref[step] = jnp.concatenate(parts, axis=0).astype(BF16)

            @pl.when(step != 0)
            def _():
                pltpu.make_async_remote_copy(
                    send_ref.at[step],
                    recv_ref.at[step],
                    send_sem,
                    recv_sem.at[step // recv_chunk],
                    device_id=moved(me, offset_of(step, dims), dims),
                    device_id_type=MESH,
                ).start()

            return carry

        return lax.fori_loop(0, send_chunk, one, carry)

    lax.fori_loop(0, 2, send_part, 0)
    drain(near_in, 1, groups - 1, near_recv)
    swapped = dot(second_ref[...], near_in[...].reshape(total, 256).astype(BF16))
    far_out[...] = swapped.reshape(far_out.shape)
    lax.fori_loop(1, others, start_all(far_copy), 0)
    far_in[0] = far_out[0]
    lax.fori_loop(2, 8, send_part, 0)
    recv_ref[0] = send_ref[0]

    drain(far_in, 1, others - 1, far_recv)
    sheet_in = far_in[...].reshape(total, 256)
    turned_ref[...] = dot(jnp.transpose(sheet_in).astype(BF16), third_ref[...])

    acc_ref[...] = jnp.zeros_like(acc_ref)
    parts = acc_ref.shape[0] // 6

    def recv_part(chunk, carry):
        base = chunk * recv_chunk

        @pl.when(chunk == 0)
        def _():
            drain(recv_ref, 1, recv_chunk - 1, recv_sem.at[0])

        @pl.when(chunk != 0)
        def _():
            drain(recv_ref, base, recv_chunk, recv_sem.at[chunk])

        lined = pltpu.roll(turned_ref[...], (total - base) % total, 1)
        for index in range(recv_chunk):
            part = lined[:, index : index + 1]
            where = pl.ds(index * CAP, CAP)
            for v in range(6):
                column_ref[v, where, :] = jnp.broadcast_to(part[32 * v : 32 * v + CAP], (CAP, LANES))
            tile = part[192 : 192 + CAP] * 256.0 + part[224 : 224 + CAP]
            column_ref[6, where, :] = jnp.broadcast_to(tile, (CAP, LANES))

        def unpack(index, carry):
            block = recv_ref[base + index].astype(F32)
            for c in range(CELLS // LANES):
                cell_ref[c, pl.ds(pl.multiple_of(index * CAP, 8), CAP), :] = block[c * CAP : (c + 1) * CAP]
            return carry

        lax.fori_loop(0, recv_chunk, unpack, 0)
        for c in range(CELLS // LANES):
            flip_ref[c * LANES : (c + 1) * LANES, :] = jnp.transpose(cell_ref[c]).astype(BF16)

        def component(q, carry):
            lane = iota((depth, LANES), 1).astype(F32)
            tile = column_ref[6]
            value = column_ref[q]
            pieces = []
            for part in range(parts):
                pieces.append(jnp.where(tile == lane + part * LANES, value, 0.0).astype(BF16))
            weight = jnp.concatenate(pieces, axis=1)
            product = dot(flip_ref[...], weight)
            for part in range(parts):
                acc_ref[q * parts + part] += product[:, part * LANES : (part + 1) * LANES]
            return carry

        return lax.fori_loop(0, 6, component, carry)

    lax.fori_loop(0, 4, recv_part, 0)
    drain(send_ref, 1, total - 1, send_sem)
    drain(near_out, 1, groups - 1, near_send)
    drain(far_out, 1, others - 1, far_send)


def gather_tiles(dims, step_row, meta, areas, tiles):
    total = dims[0] * dims[1] * dims[2] * dims[3]
    groups, others = dims[0] * dims[3], dims[1] * dims[2]
    rows = areas.shape[0]
    depth = total // 4 * CAP
    block = (total, CAP * CELLS // LANES, LANES)
    vmem = pl.BlockSpec(memory_space=pltpu.VMEM)
    return pl.pallas_call(
        functools.partial(gather_kernel, dims),
        out_shape=jax.ShapeDtypeStruct((6 * tiles // LANES, CELLS, LANES), F32),
        in_specs=[vmem] * 6,
        out_specs=vmem,
        scratch_shapes=[
            pltpu.VMEM((1, rows), F32),
            pltpu.VMEM((total // 8 * CAP, CELLS), F32),
            pltpu.VMEM(block, BF16),
            pltpu.VMEM(block, BF16),
            pltpu.VMEM((groups, others, 256), F32),
            pltpu.VMEM((groups, others, 256), F32),
            pltpu.VMEM((others, groups, 256), F32),
            pltpu.VMEM((others, groups, 256), F32),
            pltpu.VMEM((256, total), F32),
            pltpu.VMEM((7, depth, LANES), F32),
            pltpu.VMEM((CELLS // LANES, depth, LANES), F32),
            pltpu.VMEM((CELLS, depth), BF16),
            pltpu.SemaphoreType.DMA,
            pltpu.SemaphoreType.DMA((4,)),
            pltpu.SemaphoreType.DMA,
            pltpu.SemaphoreType.DMA,
            pltpu.SemaphoreType.DMA,
            pltpu.SemaphoreType.DMA,
        ],
        compiler_params=pltpu.CompilerParams(
            collective_id=0, has_side_effects=True, vmem_limit_bytes=56 << 20
        ),
    )(step_row, meta, areas, *permutations(dims))


def swap_groups(values):
    group = iota(values[0].shape, 1) // 16
    for size in (4, 2, 1):
        high = (group // size) % 2 == 1
        result = list(values)
        for i in range(8):
            if i & size == 0:
                low, up = values[i], values[i + size]
                result[i] = jnp.where(high, pltpu.roll(up, 16 * size, 1), low)
                result[i + size] = jnp.where(high, up, pltpu.roll(low, LANES - 16 * size, 1))
        values = result
    return values


def split_rows(row, out):
    lane = iota((8, LANES), 1)
    index = (lane % 16) * 8 + lane // 16
    for half in range(row.shape[1] // (8 * LANES)):
        pieces = []
        for m in range(8):
            piece = row[:, (half * 8 + m) * LANES : (half * 8 + m + 1) * LANES]
            pieces.append(jnp.take_along_axis(piece, index, axis=1))
        for l, value in enumerate(swap_groups(pieces)):
            out(l, half, value)


def join_rows(load, halves):
    lane = iota((8, LANES), 1)
    index = (lane % 8) * 16 + lane // 8
    pieces = []
    for half in range(halves):
        for value in swap_groups([load(l, half) for l in range(8)]):
            pieces.append(jnp.take_along_axis(value, index, axis=1))
    return pieces


def split_kernel(*refs):
    count = len(refs) // 2
    for source, target in zip(refs[:count], refs[count:]):
        for b in range(source.shape[1] // 8):

            def out(l, half, value, target=target, b=b):
                target[0, half, pl.ds(b * 64 + l, 8, stride=8), :] = value

            split_rows(source[0, b * 8 : (b + 1) * 8, :], out)


def split_cells(*arrays):
    nz, ny, nx = arrays[0].shape
    shape = (nz, nx // (8 * LANES), ny * 8, LANES)
    return pl.pallas_call(
        split_kernel,
        grid=(nz,),
        in_specs=[pl.BlockSpec((1, ny, nx), lambda z: (z, 0, 0))] * len(arrays),
        out_specs=[pl.BlockSpec((1,) + shape[1:], lambda z: (z, 0, 0, 0))] * len(arrays),
        out_shape=[jax.ShapeDtypeStruct(shape, F32)] * len(arrays),
        compiler_params=pltpu.CompilerParams(vmem_limit_bytes=32 << 20),
    )(*arrays)


def join_kernel(acc_ref, rock_ref, field_ref, perm_ref, pressure_ref):
    ny = rock_ref.shape[1]
    halves = rock_ref.shape[2] // (8 * LANES)
    for b in range(ny // 8):

        def load_field(l, half, b=b):
            return field_ref[0, half, pl.ds(b * 64 + l, 8, stride=8), :]

        for m, value in enumerate(join_rows(load_field, halves)):
            pressure_ref[0, b * 8 : (b + 1) * 8, m * LANES : (m + 1) * LANES] = value
        for q in range(6):

            def load(l, half, b=b, q=q):
                return acc_ref[(q * (ny // 8) + b) * halves + half, pl.ds(l, 8, stride=8), :]

            for m, value in enumerate(join_rows(load, halves)):
                at = slice(m * LANES, (m + 1) * LANES)
                if q < 3:
                    value = value + rock_ref[0, b * 8 : (b + 1) * 8, at]
                perm_ref[q, 0, b * 8 : (b + 1) * 8, at] = value


def join_cells(acc, rock, field):
    nz, ny, nx = rock.shape
    brick = pl.BlockSpec((1, ny, nx), lambda z: (z, 0, 0))
    return pl.pallas_call(
        join_kernel,
        grid=(nz,),
        in_specs=[
            pl.BlockSpec((acc.shape[0], 64, LANES), lambda z: (0, z, 0)),
            brick,
            pl.BlockSpec((1,) + field.shape[1:], lambda z: (z, 0, 0, 0)),
        ],
        out_specs=[pl.BlockSpec((6, 1, ny, nx), lambda z: (0, z, 0, 0)), brick],
        out_shape=[
            jax.ShapeDtypeStruct((6, nz, ny, nx), F32),
            jax.ShapeDtypeStruct((nz, ny, nx), F32),
        ],
        compiler_params=pltpu.CompilerParams(vmem_limit_bytes=32 << 20),
    )(acc, rock, field)


def along_x(row):
    l, c = iota(row.shape, 1), iota(row.shape, 2)
    edge = jnp.zeros((1,) + row.shape[1:], F32)
    up = pltpu.roll(row, 7, 1)
    over = pltpu.roll(up, LANES - 1, 2)
    over = jnp.where(c == LANES - 1, jnp.concatenate([over[1:], edge], axis=0), over)
    down = pltpu.roll(row, 1, 1)
    under = pltpu.roll(down, 1, 2)
    under = jnp.where(c == 0, jnp.concatenate([edge, under[:-1]], axis=0), under)
    return jnp.where(l == 7, over, up), jnp.where(l == 0, under, down)


def sweep_kernel(
    dims,
    acc_ref,
    rock_ref,
    source_ref,
    start_ref,
    field_ref,
    p_ref,
    d_ref,
    coef_ref,
    yy_ref,
    zz_ref,
    send_sem,
    recv_sem,
    coef_send,
    coef_recv,
):
    me = place(dims)
    gz_count = dims[0]
    xy_count = dims[1] * dims[2] * dims[3]
    z, h = lax.axis_index("gz"), lax.axis_index("xy")
    nz, halves, ny = rock_ref.shape[:3]
    row_shape = (halves, 8, LANES)

    def beside(dz, dh):
        return (z + dz + gz_count) % gz_count, (h + dh + xy_count) % xy_count

    sides = [(dz, dh) for dz in (-1, 0, 1) for dh in (-1, 0, 1) if dz or dh]
    barrier = pltpu.get_barrier_semaphore()
    for dz, dh in sides:
        pl.semaphore_signal(barrier, inc=1, device_id=beside(dz, dh), device_id_type=MESH)
    pl.semaphore_wait(barrier, len(sides))

    def span(d, size, halo):
        if d == 0:
            return pl.ds(1, size)
        if halo:
            return pl.ds(0, 1) if d > 0 else pl.ds(size + 1, 1)
        return pl.ds(size, 1) if d > 0 else pl.ds(1, 1)

    def copies(t):
        return [
            pltpu.make_async_remote_copy(
                p_ref.at[t, span(dz, nz, False), :, span(dh, ny, False)],
                p_ref.at[t, span(dz, nz, True), :, span(dh, ny, True)],
                send_sem.at[t, n],
                recv_sem.at[t, n],
                device_id=beside(dz, dh),
                device_id_type=MESH,
            )
            for n, (dz, dh) in enumerate(sides)
        ]

    def clear_edges(t):
        @pl.when(z == 0)
        def _():
            p_ref[t, 0] = jnp.zeros((halves, ny + 2, 8, LANES), F32)

        @pl.when(z == gz_count - 1)
        def _():
            p_ref[t, nz + 1] = jnp.zeros((halves, ny + 2, 8, LANES), F32)

        @pl.when(h == 0)
        def _():
            p_ref[t, :, :, 0] = jnp.zeros((nz + 2, halves, 8, LANES), F32)

        @pl.when(h == xy_count - 1)
        def _():
            p_ref[t, :, :, ny + 1] = jnp.zeros((nz + 2, halves, 8, LANES), F32)

    def fracture(q, i, y):
        b, j = y // 8, y % 8
        rows = pl.ds(pl.multiple_of((i * 8 + j) * 8, 8), 8)
        return acc_ref[pl.ds((q * (ny // 8) + b) * halves, halves), rows, :]

    def fill(n, carry):
        i, y = n // ny, n % ny
        rock = rock_ref[i, :, y]
        yy_ref[i, :, 1 + y] = fracture(1, i, y) + rock
        zz_ref[1 + i, :, y] = fracture(2, i, y) + rock
        p_ref[0, 1 + i, :, 1 + y] = start_ref[i, :, y]
        return carry

    lax.fori_loop(0, nz * ny, fill, 0)
    ends = []
    for n, d in enumerate((1, -1)):
        inner, outer = span(d, ny, False), span(d, ny, True)
        ends.append((yy_ref.at[:, :, inner], yy_ref.at[:, :, outer], n, (0, d)))
        inner, outer = span(d, nz, False), span(d, nz, True)
        ends.append((zz_ref.at[inner], zz_ref.at[outer], 2 + n, (d, 0)))
    coef_copies = [
        pltpu.make_async_remote_copy(
            source,
            target,
            coef_send.at[n],
            coef_recv.at[n],
            device_id=beside(*side),
            device_id_type=MESH,
        )
        for source, target, n, side in ends
    ]
    for copy in coef_copies:
        copy.start()
    for copy in copies(0):
        copy.start()
    for copy in coef_copies:
        copy.wait()

    @pl.when(z == 0)
    def _():
        zz_ref[0] = jnp.zeros((halves, ny, 8, LANES), F32)

    @pl.when(z == gz_count - 1)
    def _():
        zz_ref[nz + 1] = jnp.zeros((halves, ny, 8, LANES), F32)

    @pl.when(h == 0)
    def _():
        yy_ref[:, :, 0] = jnp.zeros((nz, halves, 8, LANES), F32)

    @pl.when(h == xy_count - 1)
    def _():
        yy_ref[:, :, ny + 1] = jnp.zeros((nz, halves, 8, LANES), F32)

    def prepare(n, carry):
        i, y = n // ny, n % ny
        k = fracture(0, i, y) + rock_ref[i, :, y]
        more, less = along_x(k)
        faces = [0.5 * (k + more), 0.5 * (k + less)]
        k = yy_ref[i, :, 1 + y]
        faces += [0.5 * (k + yy_ref[i, :, 2 + y]), 0.5 * (k + yy_ref[i, :, y])]
        k = zz_ref[1 + i, :, y]
        faces += [0.5 * (k + zz_ref[2 + i, :, y]), 0.5 * (k + zz_ref[i, :, y])]
        inverse = 1.0 / functools.reduce(lambda left, right: left + right, faces)
        for m, face in enumerate(faces):
            coef_ref[m, i, :, y] = face * inverse
        for m in range(3):
            coef_ref[6 + m, i, :, y] = fracture(3 + m, i, y) * (0.25 * inverse)
        coef_ref[9, i, :, y] = source_ref[i, :, y] * inverse
        return carry

    lax.fori_loop(0, nz * ny, prepare, 0)

    for t, weight in enumerate(STEP_WEIGHTS * SWEEPS):
        for copy in copies(t):
            copy.wait()
        clear_edges(t)

        def differ(n, carry, t=t):
            i, y = n // (ny + 2), n % (ny + 2)
            more, less = along_x(p_ref[t, i, :, y])
            d_ref[i, :, y] = more - less
            return carry

        lax.fori_loop(0, (nz + 2) * (ny + 2), differ, 0)

        def advance(n, carry, t=t, weight=weight):
            i, y = n // ny, n % ny
            p = lambda dz, dy: p_ref[t, i + 1 + dz, :, y + 1 + dy]
            d = lambda dz, dy: d_ref[i + 1 + dz, :, y + 1 + dy]
            coef = lambda m: coef_ref[m, i, :, y]
            here = p(0, 0)
            more, less = along_x(here)
            total = coef(9) + coef(0) * more + coef(1) * less
            total = total + coef(2) * p(0, 1) + coef(3) * p(0, -1)
            total = total + coef(4) * p(1, 0) + coef(5) * p(-1, 0)
            total = total + coef(6) * (d(0, 1) - d(0, -1)) + coef(7) * (d(1, 0) - d(-1, 0))
            total = total + coef(8) * ((p(1, 1) - p(-1, 1)) - (p(1, -1) - p(-1, -1)))
            value = (1.0 - weight) * here + weight * total
            if t + 1 < len(STEP_WEIGHTS) * SWEEPS:
                p_ref[t + 1, i + 1, :, y + 1] = value
            else:
                field_ref[i, :, y] = value
            return carry

        lax.fori_loop(0, nz * ny, advance, 0)
        if t + 1 < len(STEP_WEIGHTS) * SWEEPS:
            for copy in copies(t + 1):
                copy.start()


def sweep(dims, acc, rock, source, start):
    nz, halves, ny8, _ = rock.shape
    ny = ny8 // 8
    shape = (nz, halves, ny, 8, LANES)
    vmem = pl.BlockSpec(memory_space=pltpu.VMEM)
    steps = len(STEP_WEIGHTS) * SWEEPS
    field = pl.pallas_call(
        functools.partial(sweep_kernel, dims),
        out_shape=jax.ShapeDtypeStruct(shape, F32),
        in_specs=[vmem] * 4,
        out_specs=vmem,
        scratch_shapes=[
            pltpu.VMEM((steps, nz + 2, halves, ny + 2, 8, LANES), F32),
            pltpu.VMEM((nz + 2, halves, ny + 2, 8, LANES), F32),
            pltpu.VMEM((10,) + shape, F32),
            pltpu.VMEM((nz, halves, ny + 2, 8, LANES), F32),
            pltpu.VMEM((nz + 2, halves, ny, 8, LANES), F32),
            pltpu.SemaphoreType.DMA((steps, 8)),
            pltpu.SemaphoreType.DMA((steps, 8)),
            pltpu.SemaphoreType.DMA((4,)),
            pltpu.SemaphoreType.DMA((4,)),
        ],
        compiler_params=pltpu.CompilerParams(
            collective_id=1, has_side_effects=True, vmem_limit_bytes=56 << 20
        ),
    )(acc, rock.reshape(shape), source.reshape(shape), start.reshape(shape))
    return field.reshape(rock.shape)


def body(dims, areas, angles, transm, owner, tile, live_count, rock, source, start):
    rows = areas.shape[0]
    nz, nx, ny, nc = dims
    tiles = rock.size // CELLS
    mz, mx, my, mc = place(dims)
    target = owner[:, 0]
    xy = nx * ny * nc
    oz, ox, oy, oc = target // xy, (target // (ny * nc)) % nx, (target // nc) % ny, target % nc
    step = step_of((oz - mz) % nz, (ox - mx) % nx, (oy - my) % ny, (oc - mc) % nc, dims)
    live = jnp.arange(rows, dtype=jnp.int32) < live_count[0]
    step_row = jnp.where(live, step, -1).reshape(1, rows)
    high, low = tile // 256, tile % 256
    meta = jnp.concatenate(
        [tensor_rows(angles, transm), jnp.stack([high, low]).astype(F32)], axis=0
    )
    split = split_cells(rock, source, start)
    acc = gather_tiles(dims, step_row, meta, areas, tiles)
    field = sweep(dims, acc, *split)
    return tuple(join_cells(acc, rock, field))


def solution(mesh):
    return jax.shard_map(
        functools.partial(body, grid_of(mesh)),
        mesh=mesh,
        in_specs=(
            P(("gz", "xy"), None),
            P(None, ("gz", "xy")),
            P(("gz", "xy")),
            P(("gz", "xy"), None),
            P(("gz", "xy")),
            P(("gz", "xy")),
            P("gz", "xy", None),
            P("gz", "xy", None),
            P("gz", "xy", None),
        ),
        out_specs=(P(None, "gz", "xy", None), P("gz", "xy", None)),
        check_vma=False,
    )
```

```python
import functools
import math

import jax
import jax.numpy as jnp
import numpy as np
from jax import lax
from jax.experimental import pallas as pl
from jax.experimental.pallas import tpu as pltpu
from jax.sharding import PartitionSpec as P

TILE = 8
SWEEPS = 2
CAP = 24
CELLS = TILE * TILE * TILE
LANES = 128
STEP_WEIGHTS = (
    1.0 / (1.0 - 0.7 * math.cos(math.pi / 4)),
    1.0 / (1.0 + 0.7 * math.cos(math.pi / 4)),
)
MESH = pl.DeviceIdType.MESH
F32 = jnp.float32
BF16 = jnp.bfloat16


SIZES = (4, 4, 4, 2)
TOTAL = 128
GROUPS = 8
OTHERS = 16
SEND_STEPS = 16
RECV_STEPS = (32, 32, 32, 16, 16)
DEPTH = max(RECV_STEPS) * CAP
CUTS = CELLS // LANES
HALVES = 2
BANDS = 2
SOME = 4
STEPS = len(STEP_WEIGHTS) * SWEEPS


def rem(value, by):
    return lax.rem(value, jnp.int32(by))


def div(value, by):
    return lax.div(value, jnp.int32(by))


def place():
    gz, xy = lax.axis_index("gz"), lax.axis_index("xy")
    return gz, div(xy, 8), rem(div(xy, 2), 4), rem(xy, 2)


def offset_of(step):
    core, rest = step % 2, step // 2
    a, b, c = rest % 4, (rest // 4) % 4, rest // 16
    return a, (3 * a + b) % 4, (a + 2 * b + c) % 4, core


def partner(me, step):
    core, rest = rem(step, 2), div(step, 2)
    a, b, c = rem(rest, 4), rem(div(rest, 4), 4), div(rest, 16)
    x, y = rem(me[1] + 3 * a + b, 4), rem(me[2] + a + 2 * b + c, 4)
    return rem(me[0] + a, 4), x * 8 + y * 2 + rem(me[3] + core, 2)


def near_partner(me, u):
    return rem(me[0] + div(u, 2), 4), me[1] * 8 + me[2] * 2 + rem(me[3] + rem(u, 2), 2)


def far_partner(me, w):
    return me[0], rem(me[1] + div(w, 4), 4) * 8 + rem(me[2] + rem(w, 4), 4) * 2 + me[3]


def permutations():
    first, second, third = [np.zeros((TOTAL, TOTAL), np.float32) for _ in range(3)]
    for step in range(TOTAL):
        dz, dx, dy, dc = offset_of(step)
        u, w = dz * 2 + dc, dx * 4 + dy
        first[u * OTHERS + w, step] = 1
        second[w * GROUPS + u, u * OTHERS + w] = 1
        third[w * GROUPS + u, step] = 1
    return [jnp.asarray(m, BF16) for m in (first, second, third)]


def dot(a, b):
    return jnp.dot(a, b, preferred_element_type=F32)


def iota(shape, dim):
    return lax.broadcasted_iota(jnp.int32, shape, dim)


def loop(first, last, body, unroll=1):
    def step(n, carry):
        body(n)
        return carry

    lax.fori_loop(first, last, step, 0, unroll=unroll)


def row_facts(me, angles, transm, owner, tile, live):
    rows = owner.shape[1]
    dz = ((owner >> 5) - me[0]) & 3
    dx = ((owner >> 3) - me[1]) & 3
    dy = ((owner >> 1) - me[2]) & 3
    dc = (owner - me[3]) & 1
    b = (dx - 3 * dz) & 3
    c = (dy - dz - 2 * b) & 3
    step = ((c * 4 + b) * 4 + dz) * 2 + dc
    step = jnp.where(iota((1, rows), 1) < live, step, -1)
    sines, cosines = jnp.sin(angles), jnp.cos(angles)
    polar_sin = sines[0:1]
    normal_x = polar_sin * cosines[1:2]
    normal_y = polar_sin * sines[1:2]
    normal_z = cosines[0:1]
    facts = [
        transm * (1.0 - normal_x * normal_x),
        transm * (1.0 - normal_y * normal_y),
        transm * (1.0 - normal_z * normal_z),
        -transm * normal_x * normal_y,
        -transm * normal_x * normal_z,
        -transm * normal_y * normal_z,
        (tile >> 8).astype(F32),
        (tile & 255).astype(F32),
    ]
    marks = (step == iota((TOTAL, rows), 0)).astype(F32)
    width = 256
    upper = (iota((width, width), 0) <= iota((width, width), 1)).astype(BF16)
    carry = jnp.zeros((TOTAL, 1), F32)
    ranks = []
    for block in range(rows // width):
        part = marks[:, block * width : (block + 1) * width]
        running = dot(part.astype(BF16), upper) + carry
        carry = running[:, width - 1 : width]
        ranks.append(jnp.sum(running * part, axis=0, keepdims=True) - 1.0)
    rank = jnp.concatenate(ranks, axis=1)
    slot = jnp.where(step >= 0, step.astype(F32) * CAP + rank, -1.0)
    chosen = (rank == iota((32, rows), 0).astype(F32)).astype(F32)
    spread = jnp.concatenate([chosen * fact for fact in facts], axis=0).astype(BF16)
    sheet = lax.dot_general(
        marks.astype(BF16), spread, (((1,), (1,)), ((), ())), preferred_element_type=F32
    )
    return slot, sheet


def swap_groups(values):
    lane = iota(values[0].shape, 1)
    for size in (4, 2, 1):
        high = (lane // (16 * size)) % 2 == 1
        other = jnp.where(high, lane - 16 * size, lane + 16 * size)
        result = list(values)
        for i in range(8):
            if i & size == 0:
                low, up = values[i], values[i + size]
                crossed = jnp.take_along_axis(jnp.where(high, low, up), other, axis=1)
                result[i] = jnp.where(high, crossed, low)
                result[i + size] = jnp.where(high, up, crossed)
        values = result
    return values


def split_lanes(values):
    lane = iota(values[0].shape, 1)
    index = (lane % 16) * 8 + lane // 16
    return swap_groups([jnp.take_along_axis(value, index, axis=1) for value in values])


def join_lanes(values):
    lane = iota(values[0].shape, 1)
    index = (lane % 8) * 16 + lane // 8
    return [jnp.take_along_axis(value, index, axis=1) for value in swap_groups(values)]


def lanes_of(half, m):
    return slice((half * 8 + m) * LANES, (half * 8 + m + 1) * LANES)


def along_x(rows, first, last):
    shape = rows.shape
    rows = rows.reshape(shape[0], 8, 8, LANES)
    lane, l = iota(first.shape, 2), iota(rows.shape, 2)
    edge = jnp.zeros((1,) + first.shape[1:], F32)
    over = pltpu.roll(first, LANES - 1, 2)
    over = jnp.where(lane == LANES - 1, jnp.concatenate([over[1:], edge], axis=0), over)
    under = pltpu.roll(last, 1, 2)
    under = jnp.where(lane == 0, jnp.concatenate([edge, under[:-1]], axis=0), under)
    over = jnp.stack([pltpu.roll(over, 7 - k, 1) if k < 7 else over for k in range(8)], axis=1)
    under = jnp.stack([pltpu.roll(under, 8 - k, 1) if k else under for k in range(8)], axis=1)
    more = jnp.where(l == 7, over, pltpu.roll(rows, 7, 2))
    less = jnp.where(l == 0, under, pltpu.roll(rows, 1, 2))
    return more.reshape(shape), less.reshape(shape)


def along_x_faces(rows):
    lane, l = iota(rows.shape, 3), iota(rows.shape, 2)
    edge = jnp.zeros((rows.shape[0], 1) + rows.shape[2:], F32)
    up, down = pltpu.roll(rows, 7, 2), pltpu.roll(rows, 1, 2)
    over = pltpu.roll(up, LANES - 1, 3)
    over = jnp.where(lane == LANES - 1, jnp.concatenate([over[:, 1:], edge], axis=1), over)
    under = pltpu.roll(down, 1, 3)
    under = jnp.where(lane == 0, jnp.concatenate([edge, under[:, :-1]], axis=1), under)
    return jnp.where(l == 7, over, up), jnp.where(l == 0, under, down)


def at8(start, size):
    return pl.ds(start if isinstance(start, int) else pl.multiple_of(start, 8), size)


def kernel(
    angles_ref,
    transm_ref,
    owner_ref,
    tile_ref,
    live_ref,
    first_ref,
    second_ref,
    third_ref,
    areas_hbm,
    rock_hbm,
    source_hbm,
    start_hbm,
    perm_ref,
    pressure_ref,
    areas_ref,
    plain_ref,
    slot_ref,
    picked_ref,
    send_ref,
    recv_ref,
    near_out,
    near_in,
    far_out,
    far_in,
    turned_ref,
    column_ref,
    cell_ref,
    flip_ref,
    acc_ref,
    rock_ref,
    source_ref,
    p_ref,
    d_ref,
    g_ref,
    coef_ref,
    yy_ref,
    zz_ref,
    field_ref,
    load_sem,
    send_sem,
    recv_sem,
    near_send,
    near_recv,
    far_send,
    far_recv,
    halo_send,
    halo_recv,
    coef_send,
    coef_recv,
):
    me = place()
    z, h = lax.axis_index("gz"), lax.axis_index("xy")
    gz_count, xy_count = 4, 32
    nz, ny = plain_ref.shape[1], plain_ref.shape[2]

    loads = [
        pltpu.make_async_copy(source, target, load_sem.at[n])
        for n, (source, target) in enumerate((
            (areas_hbm, areas_ref),
            (rock_hbm, plain_ref.at[0]),
            (source_hbm, plain_ref.at[1]),
            (start_hbm, plain_ref.at[2]),
        ))
    ]
    for load in loads:
        load.start()

    barrier = pltpu.get_barrier_semaphore()
    loop(
        1,
        TOTAL,
        lambda step: pl.semaphore_signal(
            barrier, inc=1, device_id=partner(me, step), device_id_type=MESH
        ),
    )

    slot, sheet = row_facts(
        me, angles_ref[...], transm_ref[...], owner_ref[...], tile_ref[...], live_ref[...]
    )
    slot_ref[...] = slot
    near_out[...] = dot(first_ref[...], sheet.astype(BF16)).reshape(near_out.shape)
    rows = areas_ref.shape[0]

    def pick(chunk):
        base = chunk * SEND_STEPS
        wanted = (iota((SEND_STEPS * CAP, rows), 0) + base * CAP).astype(F32)
        chosen = (slot_ref[...] == wanted).astype(F32).astype(BF16)
        picked_ref[...] = dot(chosen, areas_ref[...])

        def pack(index):
            block = picked_ref[at8(index * CAP, CAP), :]
            parts = [block[:, c * LANES : (c + 1) * LANES] for c in range(CUTS)]
            send_ref[base + index] = jnp.concatenate(parts, axis=0).astype(BF16)

        loop(0, SEND_STEPS, pack, unroll=4)

    def send(step, part):
        pltpu.make_async_remote_copy(
            send_ref.at[step],
            recv_ref.at[step],
            send_sem,
            recv_sem.at[part],
            device_id=partner(me, step),
            device_id_type=MESH,
        ).start()

    def near_copy(u):
        pltpu.make_async_remote_copy(
            near_out.at[u],
            near_in.at[u],
            near_send,
            near_recv,
            device_id=near_partner(me, u),
            device_id_type=MESH,
        ).start()

    def far_copy(w):
        pltpu.make_async_remote_copy(
            far_out.at[w],
            far_in.at[w],
            far_send,
            far_recv,
            device_id=far_partner(me, w),
            device_id_type=MESH,
        ).start()

    def drain(ref, first, count, sem):
        part = ref.at[pl.ds(first, count)]
        pltpu.make_async_copy(part, part, sem).wait()

    loads[0].wait()
    pick(0)
    pl.semaphore_wait(barrier, TOTAL - 1)
    loop(1, SEND_STEPS, lambda step: send(step, 0))
    recv_ref[0] = send_ref[0]
    loop(1, GROUPS, near_copy)
    near_in[0] = near_out[0]

    def pick_and_send(chunk, part):
        pick(chunk)
        loop(0, SEND_STEPS, lambda index: send(chunk * SEND_STEPS + index, part))

    pick_and_send(1, 0)
    loop(2, 4, lambda chunk: pick_and_send(chunk, div(chunk, 2)))
    drain(near_in, 1, GROUPS - 1, near_recv)
    swapped = dot(second_ref[...], near_in[...].reshape(TOTAL, 256).astype(BF16))
    far_out[...] = swapped.reshape(far_out.shape)
    loop(1, OTHERS, far_copy)
    far_in[0] = far_out[0]
    loop(4, 6, lambda chunk: pick_and_send(chunk, div(chunk, 2)))
    loop(6, 8, lambda chunk: pick_and_send(chunk, chunk - 3))

    for load in loads[1:]:
        load.wait()

    def split(i):
        for n in range(3):
            spots = [(b, half) for b in range(BANDS) for half in range(HALVES)]
            pieces = []
            for m in range(8):
                parts = [plain_ref[n, i, b * 8 : (b + 1) * 8, lanes_of(half, m)] for b, half in spots]
                pieces.append(jnp.concatenate(parts, axis=0))
            for l, value in enumerate(split_lanes(pieces)):
                for k, (b, half) in enumerate(spots):
                    here = value[k * 8 : (k + 1) * 8]
                    if n == 2:
                        p_ref[0, 1 + i, half, pl.ds(8 + b * 64 + l, 8, stride=8), :] = here
                    else:
                        target = (rock_ref, source_ref)[n]
                        target[i, half, pl.ds(b * 64 + l, 8, stride=8), :] = here

    loop(0, nz, split)

    def beside(dz, dh):
        return (z + dz + gz_count) % gz_count, (h + dh + xy_count) % xy_count

    sides = [(dz, dh) for dz in (-1, 0, 1) for dh in (-1, 0, 1) if dz or dh]

    def planes(d, halo):
        if d == 0:
            return pl.ds(1, nz)
        if halo:
            return pl.ds(0, 1) if d > 0 else pl.ds(nz + 1, 1)
        return pl.ds(nz, 1) if d > 0 else pl.ds(1, 1)

    def lines(d, halo):
        if d == 0:
            return pl.ds(8, ny * 8)
        if halo:
            return pl.ds(0, 8) if d > 0 else pl.ds(ny * 8 + 8, 8)
        return pl.ds(ny * 8, 8) if d > 0 else pl.ds(8, 8)

    def halo_copy(t, n):
        dz, dh = sides[n]
        return pltpu.make_async_remote_copy(
            p_ref.at[t, planes(dz, False), :, lines(dh, False)],
            p_ref.at[t, planes(dz, True), :, lines(dh, True)],
            halo_send.at[t, n],
            halo_recv.at[t, n],
            device_id=beside(dz, dh),
            device_id_type=MESH,
        )

    for n in range(len(sides)):
        halo_copy(0, n).start()

    drain(far_in, 1, OTHERS - 1, far_recv)
    turned_ref[...] = dot(
        jnp.transpose(far_in[...].reshape(TOTAL, 256)).astype(BF16), third_ref[...]
    )
    acc_ref[...] = jnp.zeros_like(acc_ref)
    pieces = acc_ref.shape[0] // 6

    def add_rows(base, count):
        depth = count * CAP
        lined = pltpu.roll(turned_ref[...], (TOTAL - base) % TOTAL, 1)
        for index in range(count):
            part = lined[:, index : index + 1]
            where = slice(index * CAP, (index + 1) * CAP)
            for v in range(6):
                column_ref[v, where, :] = jnp.broadcast_to(part[32 * v : 32 * v + CAP], (CAP, LANES))
            number = part[192 : 192 + CAP] * 256.0 + part[224 : 224 + CAP]
            column_ref[6, where, :] = jnp.broadcast_to(number, (CAP, LANES))

        def unpack(index):
            block = recv_ref[base + index].astype(F32)
            for c in range(CUTS):
                cell_ref[c, at8(index * CAP, CAP), :] = block[c * CAP : (c + 1) * CAP]

        loop(0, count, unpack, unroll=4)
        for c in range(CUTS):
            flip_ref[c * LANES : (c + 1) * LANES, :depth] = jnp.transpose(cell_ref[c, :depth]).astype(BF16)

        def component(q):
            lane = iota((depth, LANES), 1).astype(F32)
            number = column_ref[6, :depth]
            value = column_ref[q, :depth]
            parts = [
                jnp.where(number == lane + part * LANES, value, 0.0).astype(BF16)
                for part in range(pieces)
            ]
            product = dot(flip_ref[:, :depth], jnp.concatenate(parts, axis=1))
            for part in range(pieces):
                acc_ref[q * pieces + part] += product[:, part * LANES : (part + 1) * LANES]

        loop(0, 6, component)

    base = 0
    for part, count in enumerate(RECV_STEPS):
        first = 1 if part == 0 else 0
        drain(recv_ref, base + first, count - first, recv_sem.at[part])
        add_rows(base, count)
        base += count

    def fill(n):
        i, b = div(n, BANDS), rem(n, BANDS)
        rock = rock_ref[i, :, at8(b * 64, 64), :]
        for q in range(3):
            where = pl.ds((q * BANDS + b) * HALVES, HALVES)
            value = acc_ref[where, at8(i * 64, 64), :] + rock
            acc_ref[where, at8(i * 64, 64), :] = value
            if q == 1:
                yy_ref[i, :, at8(8 + b * 64, 64), :] = value
            if q == 2:
                zz_ref[1 + i, :, at8(b * 64, 64), :] = value

    loop(0, nz * BANDS, fill)
    coef_copies = []
    for d in (1, -1):
        ends = [
            (yy_ref.at[:, :, lines(d, False)], yy_ref.at[:, :, lines(d, True)], (0, d)),
            (zz_ref.at[planes(d, False)], zz_ref.at[planes(d, True)], (d, 0)),
        ]
        for source, target, side in ends:
            n = len(coef_copies)
            coef_copies.append(
                pltpu.make_async_remote_copy(
                    source,
                    target,
                    coef_send.at[n],
                    coef_recv.at[n],
                    device_id=beside(*side),
                    device_id_type=MESH,
                )
            )
    for copy in coef_copies:
        copy.start()

    def join(i):
        per = BANDS * HALVES
        for q in range(0, 6, 2):
            values = join_lanes([
                acc_ref[q * per : (q + 2) * per, pl.ds(i * 64 + l, 8, stride=8), :].reshape(16 * per, LANES)
                for l in range(8)
            ])
            for k in range(2 * per):
                b, half = (k % per) // HALVES, k % HALVES
                for m, value in enumerate(values):
                    perm_ref[q + k // per, i, b * 8 : (b + 1) * 8, lanes_of(half, m)] = value[k * 8 : (k + 1) * 8]

    loop(0, nz, join)
    for copy in coef_copies:
        copy.wait()

    def clear(ref, index):
        ref[index] = jnp.zeros_like(ref[index])

    every = slice(None)
    low, high = slice(0, 8), slice(ny * 8 + 8, ny * 8 + 16)
    inside = slice(1, nz + 1)

    @pl.when(z == 0)
    def _():
        clear(zz_ref, 0)

    @pl.when(z == gz_count - 1)
    def _():
        clear(zz_ref, nz + 1)

    @pl.when(h == 0)
    def _():
        clear(yy_ref, (every, every, low))

    @pl.when(h == xy_count - 1)
    def _():
        clear(yy_ref, (every, every, high))

    def prepare(n):
        i, b = div(n, BANDS), rem(n, BANDS)
        here = at8(b * 64, 64)
        where = pl.ds(b * HALVES, HALVES)
        k = acc_ref[where, at8(i * 64, 64), :]
        first = acc_ref[where, pl.ds(i * 64, 8, stride=8), :]
        last = acc_ref[where, pl.ds(i * 64 + 7, 8, stride=8), :]
        more, less = along_x(k, first, last)
        faces = [0.5 * (k + more), 0.5 * (k + less)]
        k = yy_ref[i, :, at8(b * 64 + 8, 64), :]
        faces += [0.5 * (k + yy_ref[i, :, at8(b * 64 + 16, 64), :]), 0.5 * (k + yy_ref[i, :, here, :])]
        k = zz_ref[1 + i, :, here, :]
        faces += [0.5 * (k + zz_ref[2 + i, :, here, :]), 0.5 * (k + zz_ref[i, :, here, :])]
        inverse = 1.0 / functools.reduce(lambda left, right: left + right, faces)
        for m, face in enumerate(faces):
            coef_ref[m, i, :, here, :] = face * inverse
        for m in range(3):
            cross = acc_ref[pl.ds(((3 + m) * BANDS + b) * HALVES, HALVES), at8(i * 64, 64), :]
            coef_ref[6 + m, i, :, here, :] = cross * (0.25 * inverse)
        coef_ref[9, i, :, here, :] = source_ref[i, :, here, :] * inverse

    loop(0, nz * BANDS, prepare)

    for t, weight in enumerate(STEP_WEIGHTS * SWEEPS):

        def rows_along_x(i, b, t=t):
            start = 8 + b * 64
            rows = p_ref[t, i, :, at8(start, 64), :]
            first = p_ref[t, i, :, pl.ds(start, 8, stride=8), :]
            last = p_ref[t, i, :, pl.ds(start + 7, 8, stride=8), :]
            return along_x(rows, first, last)

        def inner(i):
            for b in range(BANDS):
                here = slice(b * 64, b * 64 + 64)
                more, less = rows_along_x(1 + i, b)
                d_ref[1 + i, :, 8 + b * 64 : 72 + b * 64, :] = more - less
                g_ref[i, :, here, :] = (
                    coef_ref[9, i, :, here, :]
                    + coef_ref[0, i, :, here, :] * more
                    + coef_ref[1, i, :, here, :] * less
                )

        def advance(n, t=t, weight=weight):
            i, y = div(n, ny // SOME), rem(n, ny // SOME) * SOME
            here = at8(y * 8, SOME * 8)
            p = lambda dz, dy: p_ref[t, i + 1 + dz, :, at8((y + 1 + dy) * 8, SOME * 8), :]
            d = lambda dz, dy: d_ref[i + 1 + dz, :, at8((y + 1 + dy) * 8, SOME * 8), :]
            coef = lambda m: coef_ref[m, i, :, here, :]
            total = g_ref[i, :, here, :]
            total = total + coef(2) * p(0, 1) + coef(3) * p(0, -1)
            total = total + coef(4) * p(1, 0) + coef(5) * p(-1, 0)
            total = total + coef(6) * (d(0, 1) - d(0, -1)) + coef(7) * (d(1, 0) - d(-1, 0))
            total = total + coef(8) * ((p(1, 1) - p(-1, 1)) - (p(1, -1) - p(-1, -1)))
            value = (1.0 - weight) * p(0, 0) + weight * total
            if t + 1 < STEPS:
                p_ref[t + 1, i + 1, :, at8(y * 8 + 8, SOME * 8), :] = value
            else:
                field_ref[i, :, here, :] = value

        per = ny // SOME
        loop(0, nz, inner)
        for n, side in enumerate(sides):
            if side[0] == 0:
                halo_copy(t, n).wait()

        @pl.when(h == 0)
        def _():
            clear(p_ref, (t, inside, every, low))

        @pl.when(h == xy_count - 1)
        def _():
            clear(p_ref, (t, inside, every, high))

        for line in (low, high):
            more, less = along_x_faces(p_ref[t, inside, :, line, :])
            d_ref[inside, :, line, :] = more - less
        loop(per, (nz - 1) * per, advance)
        for n, side in enumerate(sides):
            if side[0] != 0:
                halo_copy(t, n).wait()

        @pl.when(h == 0)
        def _():
            clear(p_ref, (t, 0, every, low))
            clear(p_ref, (t, nz + 1, every, low))

        @pl.when(h == xy_count - 1)
        def _():
            clear(p_ref, (t, 0, every, high))
            clear(p_ref, (t, nz + 1, every, high))

        @pl.when(z == 0)
        def _():
            clear(p_ref, (t, 0))

        @pl.when(z == gz_count - 1)
        def _():
            clear(p_ref, (t, nz + 1))

        for i in (0, nz + 1):
            for b in range(BANDS):
                more, less = rows_along_x(i, b)
                d_ref[i, :, 8 + b * 64 : 72 + b * 64, :] = more - less
        loop(0, per, advance)
        loop((nz - 1) * per, nz * per, advance)
        if t + 1 < STEPS:
            for n in range(len(sides)):
                halo_copy(t + 1, n).start()

    def finish(i):
        spots = [(b, half) for b in range(BANDS) for half in range(HALVES)]
        values = join_lanes([
            jnp.concatenate([field_ref[i, half, pl.ds(b * 64 + l, 8, stride=8), :] for b, half in spots], axis=0)
            for l in range(8)
        ])
        for k, (b, half) in enumerate(spots):
            for m, value in enumerate(values):
                pressure_ref[i, b * 8 : (b + 1) * 8, lanes_of(half, m)] = value[k * 8 : (k + 1) * 8]

    loop(0, nz, finish)
    drain(send_ref, 1, TOTAL - 1, send_sem)
    drain(near_out, 1, GROUPS - 1, near_send)
    drain(far_out, 1, OTHERS - 1, far_send)


def body(areas, angles, transm, owner, tile, live_count, rock, source, start):
    rows = areas.shape[0]
    nz, ny, nx = rock.shape
    lines = ny * 8
    vmem = pl.BlockSpec(memory_space=pltpu.VMEM)
    anywhere = pl.BlockSpec(memory_space=pl.ANY)
    block = (TOTAL, CAP * CUTS, LANES)
    brick = (nz, HALVES, lines, LANES)
    dma = pltpu.SemaphoreType.DMA
    perm, pressure = pl.pallas_call(
        kernel,
        out_shape=[
            jax.ShapeDtypeStruct((6, nz, ny, nx), F32),
            jax.ShapeDtypeStruct((nz, ny, nx), F32),
        ],
        in_specs=[vmem] * 8 + [anywhere] * 4,
        out_specs=[vmem, vmem],
        scratch_shapes=[
            pltpu.VMEM((rows, CELLS), BF16),
            pltpu.VMEM((3, nz, ny, nx), F32),
            pltpu.VMEM((1, rows), F32),
            pltpu.VMEM((SEND_STEPS * CAP, CELLS), F32),
            pltpu.VMEM(block, BF16),
            pltpu.VMEM(block, BF16),
            pltpu.VMEM((GROUPS, OTHERS, 256), F32),
            pltpu.VMEM((GROUPS, OTHERS, 256), F32),
            pltpu.VMEM((OTHERS, GROUPS, 256), F32),
            pltpu.VMEM((OTHERS, GROUPS, 256), F32),
            pltpu.VMEM((256, TOTAL), F32),
            pltpu.VMEM((7, DEPTH, LANES), F32),
            pltpu.VMEM((CUTS, DEPTH, LANES), F32),
            pltpu.VMEM((CELLS, DEPTH), BF16),
            pltpu.VMEM((6 * BANDS * HALVES, CELLS, LANES), F32),
            pltpu.VMEM(brick, F32),
            pltpu.VMEM(brick, F32),
            pltpu.VMEM((STEPS, nz + 2, HALVES, lines + 16, LANES), F32),
            pltpu.VMEM((nz + 2, HALVES, lines + 16, LANES), F32),
            pltpu.VMEM(brick, F32),
            pltpu.VMEM((10,) + brick, F32),
            pltpu.VMEM((nz, HALVES, lines + 16, LANES), F32),
            pltpu.VMEM((nz + 2, HALVES, lines, LANES), F32),
            pltpu.VMEM(brick, F32),
            dma((4,)),
            dma,
            dma((len(RECV_STEPS),)),
            dma,
            dma,
            dma,
            dma,
            dma((STEPS, 8)),
            dma((STEPS, 8)),
            dma((4,)),
            dma((4,)),
        ],
        compiler_params=pltpu.CompilerParams(
            collective_id=0, has_side_effects=True, vmem_limit_bytes=62 << 20
        ),
    )(
        angles,
        transm.reshape(1, rows),
        owner.reshape(1, rows),
        tile.reshape(1, rows),
        live_count.reshape(1, 1),
        *permutations(),
        areas,
        rock,
        source,
        start,
    )
    return perm, pressure


def solution(mesh):
    return jax.shard_map(
        body,
        mesh=mesh,
        in_specs=(
            P(("gz", "xy"), None),
            P(None, ("gz", "xy")),
            P(("gz", "xy")),
            P(("gz", "xy"), None),
            P(("gz", "xy")),
            P(("gz", "xy")),
            P("gz", "xy", None),
            P("gz", "xy", None),
            P("gz", "xy", None),
        ),
        out_specs=(P(None, "gz", "xy", None), P("gz", "xy", None)),
        check_vma=False,
    )
```

```python
import functools
import math

import jax
import jax.numpy as jnp
import numpy as np
from jax import lax
from jax.experimental import pallas as pl
from jax.experimental.pallas import tpu as pltpu
from jax.sharding import PartitionSpec as P

TILE = 8
SWEEPS = 2
CAP = 24
CELLS = TILE * TILE * TILE
LANES = 128
STEP_WEIGHTS = (
    1.0 / (1.0 - 0.7 * math.cos(math.pi / 4)),
    1.0 / (1.0 + 0.7 * math.cos(math.pi / 4)),
)
MESH = pl.DeviceIdType.MESH
F32 = jnp.float32
BF16 = jnp.bfloat16


SIZES = (4, 4, 4, 2)
TOTAL = 128
GROUPS = 8
OTHERS = 16
SEND_STEPS = 16
RECV_STEPS = (32, 32, 32, 16, 16)
DEPTH = max(RECV_STEPS) * CAP
CUTS = CELLS // LANES
HALVES = 2
BANDS = 2
SOME = 4
STEPS = len(STEP_WEIGHTS) * SWEEPS


def rem(value, by):
    return lax.rem(value, jnp.int32(by))


def div(value, by):
    return lax.div(value, jnp.int32(by))


def place():
    gz, xy = lax.axis_index("gz"), lax.axis_index("xy")
    return gz, div(xy, 8), rem(div(xy, 2), 4), rem(xy, 2)


def offset_of(step):
    core, rest = step % 2, step // 2
    a, b, c = rest % 4, (rest // 4) % 4, rest // 16
    return a, (3 * a + b) % 4, (a + 2 * b + c) % 4, core


def partner(me, step):
    core, rest = rem(step, 2), div(step, 2)
    a, b, c = rem(rest, 4), rem(div(rest, 4), 4), div(rest, 16)
    x, y = rem(me[1] + 3 * a + b, 4), rem(me[2] + a + 2 * b + c, 4)
    return rem(me[0] + a, 4), x * 8 + y * 2 + rem(me[3] + core, 2)


def near_partner(me, u):
    return rem(me[0] + div(u, 2), 4), me[1] * 8 + me[2] * 2 + rem(me[3] + rem(u, 2), 2)


def far_partner(me, w):
    return me[0], rem(me[1] + div(w, 4), 4) * 8 + rem(me[2] + rem(w, 4), 4) * 2 + me[3]


def permutations():
    first, second, third = [np.zeros((TOTAL, TOTAL), np.float32) for _ in range(3)]
    for step in range(TOTAL):
        dz, dx, dy, dc = offset_of(step)
        u, w = dz * 2 + dc, dx * 4 + dy
        first[u * OTHERS + w, step] = 1
        second[w * GROUPS + u, u * OTHERS + w] = 1
        third[w * GROUPS + u, step] = 1
    return [jnp.asarray(m, BF16) for m in (first, second, third)]


def dot(a, b):
    return jnp.dot(a, b, preferred_element_type=F32)


def iota(shape, dim):
    return lax.broadcasted_iota(jnp.int32, shape, dim)


def loop(first, last, body, unroll=1):
    def step(n, carry):
        body(n)
        return carry

    lax.fori_loop(first, last, step, 0, unroll=unroll)


def row_slots(me, owner, live):
    rows = owner.shape[1]
    dz = ((owner >> 5) - me[0]) & 3
    dx = ((owner >> 3) - me[1]) & 3
    dy = ((owner >> 1) - me[2]) & 3
    dc = (owner - me[3]) & 1
    b = (dx - 3 * dz) & 3
    c = (dy - dz - 2 * b) & 3
    step = ((c * 4 + b) * 4 + dz) * 2 + dc
    step = jnp.where(iota((1, rows), 1) < live, step, -1)
    marks = (step == iota((TOTAL, rows), 0)).astype(F32)
    width = 256
    upper = (iota((width, width), 0) <= iota((width, width), 1)).astype(BF16)
    carry = jnp.zeros((TOTAL, 1), F32)
    ranks = []
    for block in range(rows // width):
        part = marks[:, block * width : (block + 1) * width]
        running = dot(part.astype(BF16), upper) + carry
        carry = running[:, width - 1 : width]
        ranks.append(jnp.sum(running * part, axis=0, keepdims=True) - 1.0)
    return step.astype(F32), jnp.concatenate(ranks, axis=1)


def fact_sheet(step, rank, angles, transm, tile):
    rows = step.shape[1]
    sines, cosines = jnp.sin(angles), jnp.cos(angles)
    polar_sin = sines[0:1]
    normal_x = polar_sin * cosines[1:2]
    normal_y = polar_sin * sines[1:2]
    normal_z = cosines[0:1]
    facts = [
        transm * (1.0 - normal_x * normal_x),
        transm * (1.0 - normal_y * normal_y),
        transm * (1.0 - normal_z * normal_z),
        -transm * normal_x * normal_y,
        -transm * normal_x * normal_z,
        -transm * normal_y * normal_z,
        (tile >> 8).astype(F32),
        (tile & 255).astype(F32),
    ]
    marks = (step == iota((TOTAL, rows), 0).astype(F32)).astype(F32).astype(BF16)
    chosen = (rank == iota((32, rows), 0).astype(F32)).astype(F32)
    spread = jnp.concatenate([chosen * fact for fact in facts], axis=0).astype(BF16)
    return lax.dot_general(marks, spread, (((1,), (1,)), ((), ())), preferred_element_type=F32)


def swap_groups(values):
    lane = iota(values[0].shape, 1)
    for size in (4, 2, 1):
        high = (lane // (16 * size)) % 2 == 1
        other = jnp.where(high, lane - 16 * size, lane + 16 * size)
        result = list(values)
        for i in range(8):
            if i & size == 0:
                low, up = values[i], values[i + size]
                crossed = jnp.take_along_axis(jnp.where(high, low, up), other, axis=1)
                result[i] = jnp.where(high, crossed, low)
                result[i + size] = jnp.where(high, up, crossed)
        values = result
    return values


def split_lanes(values):
    lane = iota(values[0].shape, 1)
    index = (lane % 16) * 8 + lane // 16
    return swap_groups([jnp.take_along_axis(value, index, axis=1) for value in values])


def join_lanes(values):
    lane = iota(values[0].shape, 1)
    index = (lane % 8) * 16 + lane // 8
    return [jnp.take_along_axis(value, index, axis=1) for value in swap_groups(values)]


def lanes_of(half, m):
    return slice((half * 8 + m) * LANES, (half * 8 + m + 1) * LANES)


def along_x(rows, first, last):
    shape = rows.shape
    rows = rows.reshape(shape[0], 8, 8, LANES)
    lane, l = iota(first.shape, 2), iota(rows.shape, 2)
    edge = jnp.zeros((1,) + first.shape[1:], F32)
    over = pltpu.roll(first, LANES - 1, 2)
    over = jnp.where(lane == LANES - 1, jnp.concatenate([over[1:], edge], axis=0), over)
    under = pltpu.roll(last, 1, 2)
    under = jnp.where(lane == 0, jnp.concatenate([edge, under[:-1]], axis=0), under)
    over = jnp.stack([pltpu.roll(over, 7 - k, 1) if k < 7 else over for k in range(8)], axis=1)
    under = jnp.stack([pltpu.roll(under, 8 - k, 1) if k else under for k in range(8)], axis=1)
    more = jnp.where(l == 7, over, pltpu.roll(rows, 7, 2))
    less = jnp.where(l == 0, under, pltpu.roll(rows, 1, 2))
    return more.reshape(shape), less.reshape(shape)


def along_x_faces(rows):
    lane, l = iota(rows.shape, 3), iota(rows.shape, 2)
    edge = jnp.zeros((rows.shape[0], 1) + rows.shape[2:], F32)
    up, down = pltpu.roll(rows, 7, 2), pltpu.roll(rows, 1, 2)
    over = pltpu.roll(up, LANES - 1, 3)
    over = jnp.where(lane == LANES - 1, jnp.concatenate([over[:, 1:], edge], axis=1), over)
    under = pltpu.roll(down, 1, 3)
    under = jnp.where(lane == 0, jnp.concatenate([edge, under[:, :-1]], axis=1), under)
    return jnp.where(l == 7, over, up), jnp.where(l == 0, under, down)


def at8(start, size):
    return pl.ds(start if isinstance(start, int) else pl.multiple_of(start, 8), size)


def kernel(
    angles_ref,
    transm_ref,
    owner_ref,
    tile_ref,
    live_ref,
    first_ref,
    second_ref,
    third_ref,
    areas_hbm,
    rock_hbm,
    source_hbm,
    start_hbm,
    perm_out,
    pressure_out,
    perm_ref,
    pressure_ref,
    areas_ref,
    plain_ref,
    slot_ref,
    picked_ref,
    send_ref,
    recv_ref,
    near_out,
    near_in,
    far_out,
    far_in,
    turned_ref,
    column_ref,
    cell_ref,
    flip_ref,
    acc_ref,
    rock_ref,
    source_ref,
    p_ref,
    d_ref,
    g_ref,
    coef_ref,
    yy_ref,
    zz_ref,
    field_ref,
    load_sem,
    send_sem,
    recv_sem,
    near_send,
    near_recv,
    far_send,
    far_recv,
    halo_send,
    halo_recv,
    coef_send,
    coef_recv,
    ready_sem,
    out_sem,
):
    me = place()
    z, h = lax.axis_index("gz"), lax.axis_index("xy")
    gz_count, xy_count = 4, 32
    nz, ny = plain_ref.shape[1], plain_ref.shape[2]

    loads = [
        pltpu.make_async_copy(source, target, load_sem.at[n])
        for n, (source, target) in enumerate((
            (areas_hbm, areas_ref),
            (rock_hbm, plain_ref.at[0]),
            (source_hbm, plain_ref.at[1]),
            (start_hbm, plain_ref.at[2]),
        ))
    ]
    for load in loads:
        load.start()

    barrier = pltpu.get_barrier_semaphore()

    def greet(sem, to):
        pl.semaphore_signal(sem, inc=1, device_id=to, device_id_type=MESH)

    loop(1, GROUPS, lambda u: greet(barrier, near_partner(me, u)))
    loop(1, OTHERS, lambda w: greet(barrier, far_partner(me, w)))
    step, rank = row_slots(me, owner_ref[...], live_ref[...])
    slot_ref[0:1] = jnp.where(step >= 0, step * CAP + rank, -1.0)
    slot_ref[1:2] = step
    slot_ref[2:3] = rank
    rows = areas_ref.shape[0]

    def pick(chunk):
        base = chunk * SEND_STEPS
        wanted = (iota((SEND_STEPS * CAP, rows), 0) + base * CAP).astype(F32)
        chosen = (slot_ref[0:1] == wanted).astype(F32).astype(BF16)
        picked_ref[...] = dot(chosen, areas_ref[...])

        def pack(index):
            block = picked_ref[at8(index * CAP, CAP), :]
            parts = [block[:, c * LANES : (c + 1) * LANES] for c in range(CUTS)]
            send_ref[base + index] = jnp.concatenate(parts, axis=0).astype(BF16)

        loop(0, SEND_STEPS, pack, unroll=4)

    def send(step, part):
        pltpu.make_async_remote_copy(
            send_ref.at[step],
            recv_ref.at[step],
            send_sem,
            recv_sem.at[part],
            device_id=partner(me, step),
            device_id_type=MESH,
        ).start()

    def near_copy(u):
        pltpu.make_async_remote_copy(
            near_out.at[u],
            near_in.at[u],
            near_send,
            near_recv,
            device_id=near_partner(me, u),
            device_id_type=MESH,
        ).start()

    def far_copy(w):
        pltpu.make_async_remote_copy(
            far_out.at[w],
            far_in.at[w],
            far_send,
            far_recv,
            device_id=far_partner(me, w),
            device_id_type=MESH,
        ).start()

    def drain(ref, first, count, sem):
        part = ref.at[pl.ds(first, count)]
        pltpu.make_async_copy(part, part, sem).wait()

    pl.semaphore_wait(barrier, GROUPS + OTHERS - 2)
    loop(1, OTHERS, lambda w: greet(ready_sem, far_partner(me, w)))
    loads[0].wait()
    pick(0)
    sheet = fact_sheet(
        slot_ref[1:2], slot_ref[2:3], angles_ref[...], transm_ref[...], tile_ref[...]
    )
    near_out[...] = dot(first_ref[...], sheet.astype(BF16)).reshape(near_out.shape)
    pl.semaphore_wait(ready_sem, OTHERS - 1)
    loop(1, GROUPS, near_copy)
    near_in[0] = near_out[0]
    loop(1, SEND_STEPS, lambda step: send(step, 0))
    recv_ref[0] = send_ref[0]
    def pick_and_send(chunk, part):
        pick(chunk)
        loop(0, SEND_STEPS, lambda index: send(chunk * SEND_STEPS + index, part))

    pick_and_send(1, 0)
    drain(near_in, 1, GROUPS - 1, near_recv)
    swapped = dot(second_ref[...], near_in[...].reshape(TOTAL, 256).astype(BF16))
    far_out[...] = swapped.reshape(far_out.shape)
    loop(1, OTHERS, far_copy)
    far_in[0] = far_out[0]
    loop(2, 6, lambda chunk: pick_and_send(chunk, div(chunk, 2)))
    loop(6, 8, lambda chunk: pick_and_send(chunk, chunk - 3))

    for load in loads[1:]:
        load.wait()

    def split(i):
        for n in range(3):
            spots = [(b, half) for b in range(BANDS) for half in range(HALVES)]
            pieces = []
            for m in range(8):
                parts = [plain_ref[n, i, b * 8 : (b + 1) * 8, lanes_of(half, m)] for b, half in spots]
                pieces.append(jnp.concatenate(parts, axis=0))
            for l, value in enumerate(split_lanes(pieces)):
                for k, (b, half) in enumerate(spots):
                    here = value[k * 8 : (k + 1) * 8]
                    if n == 2:
                        p_ref[0, 1 + i, half, pl.ds(8 + b * 64 + l, 8, stride=8), :] = here
                    else:
                        target = (rock_ref, source_ref)[n]
                        target[i, half, pl.ds(b * 64 + l, 8, stride=8), :] = here

    loop(0, nz, split)

    def beside(dz, dh):
        return (z + dz + gz_count) % gz_count, (h + dh + xy_count) % xy_count

    sides = [(dz, dh) for dz in (-1, 0, 1) for dh in (-1, 0, 1) if dz or dh]

    def planes(d, halo):
        if d == 0:
            return pl.ds(1, nz)
        if halo:
            return pl.ds(0, 1) if d > 0 else pl.ds(nz + 1, 1)
        return pl.ds(nz, 1) if d > 0 else pl.ds(1, 1)

    def lines(d, halo):
        if d == 0:
            return pl.ds(8, ny * 8)
        if halo:
            return pl.ds(0, 8) if d > 0 else pl.ds(ny * 8 + 8, 8)
        return pl.ds(ny * 8, 8) if d > 0 else pl.ds(8, 8)

    def halo_copy(t, n):
        dz, dh = sides[n]
        return pltpu.make_async_remote_copy(
            p_ref.at[t, planes(dz, False), :, lines(dh, False)],
            p_ref.at[t, planes(dz, True), :, lines(dh, True)],
            halo_send.at[t, n],
            halo_recv.at[t, n],
            device_id=beside(dz, dh),
            device_id_type=MESH,
        )

    for n in range(len(sides)):
        halo_copy(0, n).start()

    drain(far_in, 1, OTHERS - 1, far_recv)
    turned_ref[...] = dot(
        jnp.transpose(far_in[...].reshape(TOTAL, 256)).astype(BF16), third_ref[...]
    )
    acc_ref[...] = jnp.zeros_like(acc_ref)
    pieces = acc_ref.shape[0] // 6

    def list_columns(base, count):
        lined = pltpu.roll(turned_ref[...], (TOTAL - base) % TOTAL, 1)
        for index in range(count):
            part = lined[:, index : index + 1]
            where = slice(index * CAP, (index + 1) * CAP)
            for v in range(6):
                column_ref[v, where, :] = jnp.broadcast_to(part[32 * v : 32 * v + CAP], (CAP, LANES))
            number = part[192 : 192 + CAP] * 256.0 + part[224 : 224 + CAP]
            column_ref[6, where, :] = jnp.broadcast_to(number, (CAP, LANES))

    def add_rows(base, count):
        depth = count * CAP

        def unpack(index):
            block = recv_ref[base + index].astype(F32)
            for c in range(CUTS):
                cell_ref[c, at8(index * CAP, CAP), :] = block[c * CAP : (c + 1) * CAP]

        loop(0, count, unpack, unroll=4)
        for c in range(CUTS):
            flip_ref[c * LANES : (c + 1) * LANES, :depth] = jnp.transpose(cell_ref[c, :depth]).astype(BF16)

        def component(q):
            lane = iota((depth, LANES), 1).astype(F32)
            number = column_ref[6, :depth]
            value = column_ref[q, :depth]
            parts = [
                jnp.where(number == lane + part * LANES, value, 0.0).astype(BF16)
                for part in range(pieces)
            ]
            product = dot(flip_ref[:, :depth], jnp.concatenate(parts, axis=1))
            for part in range(pieces):
                acc_ref[q * pieces + part] += product[:, part * LANES : (part + 1) * LANES]

        loop(0, 6, component, unroll=2)

    base = 0
    for part, count in enumerate(RECV_STEPS):
        first = 1 if part == 0 else 0
        list_columns(base, count)
        drain(recv_ref, base + first, count - first, recv_sem.at[part])
        add_rows(base, count)
        base += count

    def fill(n):
        i, b = div(n, BANDS), rem(n, BANDS)
        rock = rock_ref[i, :, at8(b * 64, 64), :]
        for q in range(3):
            where = pl.ds((q * BANDS + b) * HALVES, HALVES)
            value = acc_ref[where, at8(i * 64, 64), :] + rock
            acc_ref[where, at8(i * 64, 64), :] = value
            if q == 1:
                yy_ref[i, :, at8(8 + b * 64, 64), :] = value
            if q == 2:
                zz_ref[1 + i, :, at8(b * 64, 64), :] = value

    loop(0, nz * BANDS, fill)
    coef_copies = []
    for d in (1, -1):
        ends = [
            (yy_ref.at[:, :, lines(d, False)], yy_ref.at[:, :, lines(d, True)], (0, d)),
            (zz_ref.at[planes(d, False)], zz_ref.at[planes(d, True)], (d, 0)),
        ]
        for source, target, side in ends:
            n = len(coef_copies)
            coef_copies.append(
                pltpu.make_async_remote_copy(
                    source,
                    target,
                    coef_send.at[n],
                    coef_recv.at[n],
                    device_id=beside(*side),
                    device_id_type=MESH,
                )
            )
    for copy in coef_copies:
        copy.start()

    def join(i, q):
        per = BANDS * HALVES
        values = join_lanes([
            acc_ref[q * per : (q + 2) * per, pl.ds(i * 64 + l, 8, stride=8), :].reshape(16 * per, LANES)
            for l in range(8)
        ])
        for k in range(2 * per):
            b, half = (k % per) // HALVES, k % HALVES
            for m, value in enumerate(values):
                perm_ref[q + k // per, i, b * 8 : (b + 1) * 8, lanes_of(half, m)] = value[k * 8 : (k + 1) * 8]

    out_copies = [
        pltpu.make_async_copy(perm_ref.at[q : q + 2], perm_out.at[q : q + 2], out_sem.at[q // 2])
        for q in (0, 2, 4)
    ] + [pltpu.make_async_copy(pressure_ref, pressure_out, out_sem.at[3])]
    loop(0, nz, lambda i: join(i, 0))
    out_copies[0].start()
    loop(0, nz // 2, lambda i: join(i, 2))
    for copy in coef_copies:
        copy.wait()

    def clear(ref, index):
        ref[index] = jnp.zeros_like(ref[index])

    every = slice(None)
    low, high = slice(0, 8), slice(ny * 8 + 8, ny * 8 + 16)
    inside = slice(1, nz + 1)

    @pl.when(z == 0)
    def _():
        clear(zz_ref, 0)

    @pl.when(z == gz_count - 1)
    def _():
        clear(zz_ref, nz + 1)

    @pl.when(h == 0)
    def _():
        clear(yy_ref, (every, every, low))

    @pl.when(h == xy_count - 1)
    def _():
        clear(yy_ref, (every, every, high))

    def prepare(n):
        i, b = div(n, BANDS), rem(n, BANDS)
        here = at8(b * 64, 64)
        where = pl.ds(b * HALVES, HALVES)
        k = acc_ref[where, at8(i * 64, 64), :]
        first = acc_ref[where, pl.ds(i * 64, 8, stride=8), :]
        last = acc_ref[where, pl.ds(i * 64 + 7, 8, stride=8), :]
        more, less = along_x(k, first, last)
        faces = [0.5 * (k + more), 0.5 * (k + less)]
        k = yy_ref[i, :, at8(b * 64 + 8, 64), :]
        faces += [0.5 * (k + yy_ref[i, :, at8(b * 64 + 16, 64), :]), 0.5 * (k + yy_ref[i, :, here, :])]
        k = zz_ref[1 + i, :, here, :]
        faces += [0.5 * (k + zz_ref[2 + i, :, here, :]), 0.5 * (k + zz_ref[i, :, here, :])]
        inverse = 1.0 / functools.reduce(lambda left, right: left + right, faces)
        for m, face in enumerate(faces):
            coef_ref[m, i, :, here, :] = face * inverse
        for m in range(3):
            cross = acc_ref[pl.ds(((3 + m) * BANDS + b) * HALVES, HALVES), at8(i * 64, 64), :]
            coef_ref[6 + m, i, :, here, :] = cross * (0.25 * inverse)
        coef_ref[9, i, :, here, :] = source_ref[i, :, here, :] * inverse

    loop(0, nz * BANDS, prepare)

    for t, weight in enumerate(STEP_WEIGHTS * SWEEPS):

        def rows_along_x(i, b, t=t):
            start = 8 + b * 64
            rows = p_ref[t, i, :, at8(start, 64), :]
            first = p_ref[t, i, :, pl.ds(start, 8, stride=8), :]
            last = p_ref[t, i, :, pl.ds(start + 7, 8, stride=8), :]
            return along_x(rows, first, last)

        def inner(i):
            for b in range(BANDS):
                here = slice(b * 64, b * 64 + 64)
                more, less = rows_along_x(1 + i, b)
                d_ref[1 + i, :, 8 + b * 64 : 72 + b * 64, :] = more - less
                g_ref[i, :, here, :] = (
                    coef_ref[9, i, :, here, :]
                    + coef_ref[0, i, :, here, :] * more
                    + coef_ref[1, i, :, here, :] * less
                )

        def advance(n, t=t, weight=weight):
            i, y = div(n, ny // SOME), rem(n, ny // SOME) * SOME
            here = at8(y * 8, SOME * 8)
            p = lambda dz, dy: p_ref[t, i + 1 + dz, :, at8((y + 1 + dy) * 8, SOME * 8), :]
            d = lambda dz, dy: d_ref[i + 1 + dz, :, at8((y + 1 + dy) * 8, SOME * 8), :]
            coef = lambda m: coef_ref[m, i, :, here, :]
            total = g_ref[i, :, here, :]
            total = total + coef(2) * p(0, 1) + coef(3) * p(0, -1)
            total = total + coef(4) * p(1, 0) + coef(5) * p(-1, 0)
            total = total + coef(6) * (d(0, 1) - d(0, -1)) + coef(7) * (d(1, 0) - d(-1, 0))
            total = total + coef(8) * ((p(1, 1) - p(-1, 1)) - (p(1, -1) - p(-1, -1)))
            value = (1.0 - weight) * p(0, 0) + weight * total
            if t + 1 < STEPS:
                p_ref[t + 1, i + 1, :, at8(y * 8 + 8, SOME * 8), :] = value
            else:
                field_ref[i, :, here, :] = value

        per = ny // SOME
        loop(0, nz, inner)
        if t:
            loop(t * 2 - 2, t * 2, lambda i: join(i, 4))
        for n, side in enumerate(sides):
            if side[0] == 0:
                halo_copy(t, n).wait()

        @pl.when(h == 0)
        def _():
            clear(p_ref, (t, inside, every, low))

        @pl.when(h == xy_count - 1)
        def _():
            clear(p_ref, (t, inside, every, high))

        for line in (low, high):
            more, less = along_x_faces(p_ref[t, inside, :, line, :])
            d_ref[inside, :, line, :] = more - less
        loop(per, (nz - 1) * per, advance)
        if t == 1:
            loop(nz // 2, nz, lambda i: join(i, 2))
            out_copies[1].start()
        if t == 2:
            loop(nz - 2, nz, lambda i: join(i, 4))
        if t == 3:
            out_copies[2].start()
        for n, side in enumerate(sides):
            if side[0] != 0:
                halo_copy(t, n).wait()

        @pl.when(h == 0)
        def _():
            clear(p_ref, (t, 0, every, low))
            clear(p_ref, (t, nz + 1, every, low))

        @pl.when(h == xy_count - 1)
        def _():
            clear(p_ref, (t, 0, every, high))
            clear(p_ref, (t, nz + 1, every, high))

        @pl.when(z == 0)
        def _():
            clear(p_ref, (t, 0))

        @pl.when(z == gz_count - 1)
        def _():
            clear(p_ref, (t, nz + 1))

        for i in (0, nz + 1):
            for b in range(BANDS):
                more, less = rows_along_x(i, b)
                d_ref[i, :, 8 + b * 64 : 72 + b * 64, :] = more - less
        loop(0, per, advance)
        loop((nz - 1) * per, nz * per, advance)
        if t + 1 < STEPS:
            for n in range(len(sides)):
                halo_copy(t + 1, n).start()

    def finish(i):
        spots = [(b, half) for b in range(BANDS) for half in range(HALVES)]
        values = join_lanes([
            jnp.concatenate([field_ref[i, half, pl.ds(b * 64 + l, 8, stride=8), :] for b, half in spots], axis=0)
            for l in range(8)
        ])
        for k, (b, half) in enumerate(spots):
            for m, value in enumerate(values):
                pressure_ref[i, b * 8 : (b + 1) * 8, lanes_of(half, m)] = value[k * 8 : (k + 1) * 8]

    loop(0, nz, finish)
    out_copies[3].start()
    for copy in out_copies:
        copy.wait()
    drain(send_ref, 1, TOTAL - 1, send_sem)
    drain(near_out, 1, GROUPS - 1, near_send)
    drain(far_out, 1, OTHERS - 1, far_send)


def export_kernel(perm_ref, pressure_ref, perm_out, pressure_out, sems):
    copies = [
        pltpu.make_async_copy(perm_ref.at[q], perm_out.at[q], sems.at[q]) for q in range(6)
    ] + [pltpu.make_async_copy(pressure_ref, pressure_out, sems.at[6])]
    for copy in copies:
        copy.start()
    for copy in copies:
        copy.wait()


def body(areas, angles, transm, owner, tile, live_count, rock, source, start):
    rows = areas.shape[0]
    nz, ny, nx = rock.shape
    lines = ny * 8
    vmem = pl.BlockSpec(memory_space=pltpu.VMEM)
    anywhere = pl.BlockSpec(memory_space=pl.ANY)
    block = (TOTAL, CAP * CUTS, LANES)
    brick = (nz, HALVES, lines, LANES)
    dma = pltpu.SemaphoreType.DMA
    perm, pressure = pl.pallas_call(
        kernel,
        out_shape=[
            jax.ShapeDtypeStruct((6, nz, ny, nx), F32),
            jax.ShapeDtypeStruct((nz, ny, nx), F32),
        ],
        in_specs=[vmem] * 8 + [anywhere] * 4,
        out_specs=[anywhere, anywhere],
        scratch_shapes=[
            pltpu.VMEM((6, nz, ny, nx), F32),
            pltpu.VMEM((nz, ny, nx), F32),
            pltpu.VMEM((rows, CELLS), BF16),
            pltpu.VMEM((3, nz, ny, nx), F32),
            pltpu.VMEM((8, rows), F32),
            pltpu.VMEM((SEND_STEPS * CAP, CELLS), F32),
            pltpu.VMEM(block, BF16),
            pltpu.VMEM(block, BF16),
            pltpu.VMEM((GROUPS, OTHERS, 256), F32),
            pltpu.VMEM((GROUPS, OTHERS, 256), F32),
            pltpu.VMEM((OTHERS, GROUPS, 256), F32),
            pltpu.VMEM((OTHERS, GROUPS, 256), F32),
            pltpu.VMEM((256, TOTAL), F32),
            pltpu.VMEM((7, DEPTH, LANES), F32),
            pltpu.VMEM((CUTS, DEPTH, LANES), F32),
            pltpu.VMEM((CELLS, DEPTH), BF16),
            pltpu.VMEM((6 * BANDS * HALVES, CELLS, LANES), F32),
            pltpu.VMEM(brick, F32),
            pltpu.VMEM(brick, F32),
            pltpu.VMEM((STEPS, nz + 2, HALVES, lines + 16, LANES), F32),
            pltpu.VMEM((nz + 2, HALVES, lines + 16, LANES), F32),
            pltpu.VMEM(brick, F32),
            pltpu.VMEM((10,) + brick, F32),
            pltpu.VMEM((nz, HALVES, lines + 16, LANES), F32),
            pltpu.VMEM((nz + 2, HALVES, lines, LANES), F32),
            pltpu.VMEM(brick, F32),
            dma((4,)),
            dma,
            dma((len(RECV_STEPS),)),
            dma,
            dma,
            dma,
            dma,
            dma((STEPS, 8)),
            dma((STEPS, 8)),
            dma((4,)),
            dma((4,)),
            pltpu.SemaphoreType.REGULAR,
            dma((4,)),
        ],
        compiler_params=pltpu.CompilerParams(
            collective_id=0, has_side_effects=True, vmem_limit_bytes=62 << 20
        ),
    )(
        angles,
        transm.reshape(1, rows),
        owner.reshape(1, rows),
        tile.reshape(1, rows),
        live_count.reshape(1, 1),
        *permutations(),
        areas,
        rock,
        source,
        start,
    )
    return tuple(
        pl.pallas_call(
            export_kernel,
            out_shape=[jax.ShapeDtypeStruct(value.shape, F32) for value in (perm, pressure)],
            in_specs=[anywhere, anywhere],
            out_specs=[anywhere, anywhere],
            scratch_shapes=[dma((7,))],
            compiler_params=pltpu.CompilerParams(vmem_limit_bytes=62 << 20),
        )(perm, pressure)
    )


def solution(mesh):
    return jax.shard_map(
        body,
        mesh=mesh,
        in_specs=(
            P(("gz", "xy"), None),
            P(None, ("gz", "xy")),
            P(("gz", "xy")),
            P(("gz", "xy"), None),
            P(("gz", "xy")),
            P(("gz", "xy")),
            P("gz", "xy", None),
            P("gz", "xy", None),
            P("gz", "xy", None),
        ),
        out_specs=(P(None, "gz", "xy", None), P("gz", "xy", None)),
        check_vma=False,
    )
```

```python
import functools
import math

import jax
import jax.numpy as jnp
import numpy as np
from jax import lax
from jax.experimental import pallas as pl
from jax.experimental.pallas import tpu as pltpu
from jax.sharding import PartitionSpec as P

TILE = 8
SWEEPS = 2
CAP = 24
CELLS = TILE * TILE * TILE
LANES = 128
STEP_WEIGHTS = (
    1.0 / (1.0 - 0.7 * math.cos(math.pi / 4)),
    1.0 / (1.0 + 0.7 * math.cos(math.pi / 4)),
)
MESH = pl.DeviceIdType.MESH
F32 = jnp.float32
BF16 = jnp.bfloat16


SIZES = (4, 4, 4, 2)
TOTAL = 128
GROUPS = 8
OTHERS = 16
SEND_STEPS = 16
RECV_STEPS = (32, 32, 32, 16, 16)
DEPTH = max(RECV_STEPS) * CAP
CUTS = CELLS // LANES
HALVES = 2
BANDS = 2
SOME = 4
LIMIT = 56
STEPS = len(STEP_WEIGHTS) * SWEEPS


def rem(value, by):
    return lax.rem(value, jnp.int32(by))


def div(value, by):
    return lax.div(value, jnp.int32(by))


def place():
    gz, xy = lax.axis_index("gz"), lax.axis_index("xy")
    return gz, div(xy, 8), rem(div(xy, 2), 4), rem(xy, 2)


def offset_of(step):
    core, rest = step % 2, step // 2
    a, b, c = rest % 4, (rest // 4) % 4, rest // 16
    return a, (3 * a + b) % 4, (a + 2 * b + c) % 4, core


def partner(me, step):
    core, rest = rem(step, 2), div(step, 2)
    a, b, c = rem(rest, 4), rem(div(rest, 4), 4), div(rest, 16)
    x, y = rem(me[1] + 3 * a + b, 4), rem(me[2] + a + 2 * b + c, 4)
    return rem(me[0] + a, 4), x * 8 + y * 2 + rem(me[3] + core, 2)


def near_partner(me, u):
    return rem(me[0] + div(u, 2), 4), me[1] * 8 + me[2] * 2 + rem(me[3] + rem(u, 2), 2)


def far_partner(me, w):
    return me[0], rem(me[1] + div(w, 4), 4) * 8 + rem(me[2] + rem(w, 4), 4) * 2 + me[3]


def permutations():
    first, second, third = [np.zeros((TOTAL, TOTAL), np.float32) for _ in range(3)]
    for step in range(TOTAL):
        dz, dx, dy, dc = offset_of(step)
        u, w = dz * 2 + dc, dx * 4 + dy
        first[u * OTHERS + w, step] = 1
        second[w * GROUPS + u, u * OTHERS + w] = 1
        third[w * GROUPS + u, step] = 1
    return [jnp.asarray(m, BF16) for m in (first, second, third)]


def dot(a, b):
    return jnp.dot(a, b, preferred_element_type=F32)


def iota(shape, dim):
    return lax.broadcasted_iota(jnp.int32, shape, dim)


def loop(first, last, body, unroll=1):
    def step(n, carry):
        body(n)
        return carry

    lax.fori_loop(first, last, step, 0, unroll=unroll)


def row_slots(me, owner, live):
    rows = owner.shape[1]
    dz = ((owner >> 5) - me[0]) & 3
    dx = ((owner >> 3) - me[1]) & 3
    dy = ((owner >> 1) - me[2]) & 3
    dc = (owner - me[3]) & 1
    b = (dx - 3 * dz) & 3
    c = (dy - dz - 2 * b) & 3
    step = ((c * 4 + b) * 4 + dz) * 2 + dc
    step = jnp.where(iota((1, rows), 1) < live, step, -1)
    marks = (step == iota((TOTAL, rows), 0)).astype(F32)
    width = 256
    upper = (iota((width, width), 0) <= iota((width, width), 1)).astype(BF16)
    carry = jnp.zeros((TOTAL, 1), F32)
    ranks = []
    for block in range(rows // width):
        part = marks[:, block * width : (block + 1) * width]
        running = dot(part.astype(BF16), upper) + carry
        carry = running[:, width - 1 : width]
        ranks.append(jnp.sum(running * part, axis=0, keepdims=True) - 1.0)
    return step.astype(F32), jnp.concatenate(ranks, axis=1)


def fact_sheet(step, rank, angles, transm, tile):
    rows = step.shape[1]
    sines, cosines = jnp.sin(angles), jnp.cos(angles)
    polar_sin = sines[0:1]
    normal_x = polar_sin * cosines[1:2]
    normal_y = polar_sin * sines[1:2]
    normal_z = cosines[0:1]
    facts = [
        transm * (1.0 - normal_x * normal_x),
        transm * (1.0 - normal_y * normal_y),
        transm * (1.0 - normal_z * normal_z),
        -transm * normal_x * normal_y,
        -transm * normal_x * normal_z,
        -transm * normal_y * normal_z,
        (tile >> 8).astype(F32),
        (tile & 255).astype(F32),
    ]
    marks = (step == iota((TOTAL, rows), 0).astype(F32)).astype(F32).astype(BF16)
    chosen = (rank == iota((32, rows), 0).astype(F32)).astype(F32)
    spread = jnp.concatenate([chosen * fact for fact in facts], axis=0).astype(BF16)
    return lax.dot_general(marks, spread, (((1,), (1,)), ((), ())), preferred_element_type=F32)


def swap_groups(values):
    lane = iota(values[0].shape, 1)
    for size in (4, 2, 1):
        high = (lane // (16 * size)) % 2 == 1
        other = jnp.where(high, lane - 16 * size, lane + 16 * size)
        result = list(values)
        for i in range(8):
            if i & size == 0:
                low, up = values[i], values[i + size]
                crossed = jnp.take_along_axis(jnp.where(high, low, up), other, axis=1)
                result[i] = jnp.where(high, crossed, low)
                result[i + size] = jnp.where(high, up, crossed)
        values = result
    return values


def split_lanes(values):
    lane = iota(values[0].shape, 1)
    index = (lane % 16) * 8 + lane // 16
    return swap_groups([jnp.take_along_axis(value, index, axis=1) for value in values])


def join_lanes(values):
    lane = iota(values[0].shape, 1)
    index = (lane % 8) * 16 + lane // 8
    return [jnp.take_along_axis(value, index, axis=1) for value in swap_groups(values)]


def lanes_of(half, m):
    return slice((half * 8 + m) * LANES, (half * 8 + m + 1) * LANES)


def along_x(rows, first, last):
    shape = rows.shape
    rows = rows.reshape(shape[0], 8, 8, LANES)
    lane, l = iota(first.shape, 2), iota(rows.shape, 2)
    edge = jnp.zeros((1,) + first.shape[1:], F32)
    over = pltpu.roll(first, LANES - 1, 2)
    over = jnp.where(lane == LANES - 1, jnp.concatenate([over[1:], edge], axis=0), over)
    under = pltpu.roll(last, 1, 2)
    under = jnp.where(lane == 0, jnp.concatenate([edge, under[:-1]], axis=0), under)
    over = jnp.stack([pltpu.roll(over, 7 - k, 1) if k < 7 else over for k in range(8)], axis=1)
    under = jnp.stack([pltpu.roll(under, 8 - k, 1) if k else under for k in range(8)], axis=1)
    more = jnp.where(l == 7, over, pltpu.roll(rows, 7, 2))
    less = jnp.where(l == 0, under, pltpu.roll(rows, 1, 2))
    return more.reshape(shape), less.reshape(shape)


def along_x_faces(rows):
    lane, l = iota(rows.shape, 3), iota(rows.shape, 2)
    edge = jnp.zeros((rows.shape[0], 1) + rows.shape[2:], F32)
    up, down = pltpu.roll(rows, 7, 2), pltpu.roll(rows, 1, 2)
    over = pltpu.roll(up, LANES - 1, 3)
    over = jnp.where(lane == LANES - 1, jnp.concatenate([over[:, 1:], edge], axis=1), over)
    under = pltpu.roll(down, 1, 3)
    under = jnp.where(lane == 0, jnp.concatenate([edge, under[:, :-1]], axis=1), under)
    return jnp.where(l == 7, over, up), jnp.where(l == 0, under, down)


def at8(start, size):
    return pl.ds(start if isinstance(start, int) else pl.multiple_of(start, 8), size)


def kernel(
    angles_ref,
    transm_ref,
    owner_ref,
    tile_ref,
    live_ref,
    first_ref,
    second_ref,
    third_ref,
    areas_hbm,
    rock_hbm,
    source_hbm,
    start_hbm,
    perm_ref,
    pressure_ref,
    slot_ref,
    send_ref,
    recv_ref,
    near_out,
    near_in,
    far_out,
    far_in,
    turned_ref,
    acc_ref,
    rock_ref,
    source_ref,
    p_ref,
    yy_ref,
    zz_ref,
    load_sem,
    send_sem,
    recv_sem,
    near_send,
    near_recv,
    far_send,
    far_recv,
    halo_send,
    halo_recv,
    coef_send,
    coef_recv,
    ready_sem,
):
    me = place()
    z, h = lax.axis_index("gz"), lax.axis_index("xy")
    gz_count, xy_count = 4, 32
    nz, ny = rock_ref.shape[0], rock_ref.shape[2] // 8

    def beside(dz, dh):
        return (z + dz + gz_count) % gz_count, (h + dh + xy_count) % xy_count

    sides = [(dz, dh) for dz in (-1, 0, 1) for dh in (-1, 0, 1) if dz or dh]

    def planes(d, halo):
        if d == 0:
            return pl.ds(1, nz)
        if halo:
            return pl.ds(0, 1) if d > 0 else pl.ds(nz + 1, 1)
        return pl.ds(nz, 1) if d > 0 else pl.ds(1, 1)

    def lines(d, halo):
        if d == 0:
            return pl.ds(8, ny * 8)
        if halo:
            return pl.ds(0, 8) if d > 0 else pl.ds(ny * 8 + 8, 8)
        return pl.ds(ny * 8, 8) if d > 0 else pl.ds(8, 8)

    def halo_copy(t, n):
        dz, dh = sides[n]
        return pltpu.make_async_remote_copy(
            p_ref.at[t, planes(dz, False), :, lines(dh, False)],
            p_ref.at[t, planes(dz, True), :, lines(dh, True)],
            halo_send.at[t, n],
            halo_recv.at[t, n],
            device_id=beside(dz, dh),
            device_id_type=MESH,
        )

    def drain(ref, first, count, sem):
        part = ref.at[pl.ds(first, count)]
        pltpu.make_async_copy(part, part, sem).wait()

    def collect(areas_ref, plain_ref, picked_ref, column_ref, cell_ref, flip_ref):
        loads = [
            pltpu.make_async_copy(source, target, load_sem.at[n])
            for n, (source, target) in enumerate((
                (areas_hbm, areas_ref),
                (rock_hbm, plain_ref.at[0]),
                (source_hbm, plain_ref.at[1]),
                (start_hbm, plain_ref.at[2]),
            ))
        ]
        for load in loads:
            load.start()

        barrier = pltpu.get_barrier_semaphore()

        def greet(sem, to):
            pl.semaphore_signal(sem, inc=1, device_id=to, device_id_type=MESH)

        loop(1, GROUPS, lambda u: greet(barrier, near_partner(me, u)))
        loop(1, OTHERS, lambda w: greet(barrier, far_partner(me, w)))
        step, rank = row_slots(me, owner_ref[...], live_ref[...])
        slot_ref[0:1] = jnp.where(step >= 0, step * CAP + rank, -1.0)
        slot_ref[1:2] = step
        slot_ref[2:3] = rank
        rows = areas_ref.shape[0]

        def pick(chunk):
            base = chunk * SEND_STEPS
            wanted = (iota((SEND_STEPS * CAP, rows), 0) + base * CAP).astype(F32)
            chosen = (slot_ref[0:1] == wanted).astype(F32).astype(BF16)
            picked_ref[...] = dot(chosen, areas_ref[...])

            def pack(index):
                block = picked_ref[at8(index * CAP, CAP), :]
                parts = [block[:, c * LANES : (c + 1) * LANES] for c in range(CUTS)]
                send_ref[base + index] = jnp.concatenate(parts, axis=0).astype(BF16)

            loop(0, SEND_STEPS, pack, unroll=4)

        def send(step, part):
            pltpu.make_async_remote_copy(
                send_ref.at[step],
                recv_ref.at[step],
                send_sem,
                recv_sem.at[part],
                device_id=partner(me, step),
                device_id_type=MESH,
            ).start()

        def near_copy(u):
            pltpu.make_async_remote_copy(
                near_out.at[u],
                near_in.at[u],
                near_send,
                near_recv,
                device_id=near_partner(me, u),
                device_id_type=MESH,
            ).start()

        def far_copy(w):
            pltpu.make_async_remote_copy(
                far_out.at[w],
                far_in.at[w],
                far_send,
                far_recv,
                device_id=far_partner(me, w),
                device_id_type=MESH,
            ).start()

        pl.semaphore_wait(barrier, GROUPS + OTHERS - 2)
        loop(1, OTHERS, lambda w: greet(ready_sem, far_partner(me, w)))
        loads[0].wait()
        pick(0)
        sheet = fact_sheet(
            slot_ref[1:2], slot_ref[2:3], angles_ref[...], transm_ref[...], tile_ref[...]
        )
        near_out[...] = dot(first_ref[...], sheet.astype(BF16)).reshape(near_out.shape)
        pl.semaphore_wait(ready_sem, OTHERS - 1)
        loop(1, GROUPS, near_copy)
        near_in[0] = near_out[0]
        loop(1, SEND_STEPS, lambda step: send(step, 0))
        recv_ref[0] = send_ref[0]
        def pick_and_send(chunk, part):
            pick(chunk)
            loop(0, SEND_STEPS, lambda index: send(chunk * SEND_STEPS + index, part))

        pick_and_send(1, 0)
        drain(near_in, 1, GROUPS - 1, near_recv)
        swapped = dot(second_ref[...], near_in[...].reshape(TOTAL, 256).astype(BF16))
        far_out[...] = swapped.reshape(far_out.shape)
        loop(1, OTHERS, far_copy)
        far_in[0] = far_out[0]
        loop(2, 6, lambda chunk: pick_and_send(chunk, div(chunk, 2)))
        loop(6, 8, lambda chunk: pick_and_send(chunk, chunk - 3))

        for load in loads[1:]:
            load.wait()

        def split(i):
            for n in range(3):
                spots = [(b, half) for b in range(BANDS) for half in range(HALVES)]
                pieces = []
                for m in range(8):
                    parts = [plain_ref[n, i, b * 8 : (b + 1) * 8, lanes_of(half, m)] for b, half in spots]
                    pieces.append(jnp.concatenate(parts, axis=0))
                for l, value in enumerate(split_lanes(pieces)):
                    for k, (b, half) in enumerate(spots):
                        here = value[k * 8 : (k + 1) * 8]
                        if n == 2:
                            p_ref[0, 1 + i, half, pl.ds(8 + b * 64 + l, 8, stride=8), :] = here
                        else:
                            target = (rock_ref, source_ref)[n]
                            target[i, half, pl.ds(b * 64 + l, 8, stride=8), :] = here

        loop(0, nz, split)

        for n in range(len(sides)):
            halo_copy(0, n).start()

        drain(far_in, 1, OTHERS - 1, far_recv)
        turned_ref[...] = dot(
            jnp.transpose(far_in[...].reshape(TOTAL, 256)).astype(BF16), third_ref[...]
        )
        acc_ref[...] = jnp.zeros_like(acc_ref)
        pieces = acc_ref.shape[0] // 6

        def list_columns(base, count):
            lined = pltpu.roll(turned_ref[...], (TOTAL - base) % TOTAL, 1)
            for index in range(count):
                part = lined[:, index : index + 1]
                where = slice(index * CAP, (index + 1) * CAP)
                for v in range(6):
                    column_ref[v, where, :] = jnp.broadcast_to(part[32 * v : 32 * v + CAP], (CAP, LANES))
                number = part[192 : 192 + CAP] * 256.0 + part[224 : 224 + CAP]
                column_ref[6, where, :] = jnp.broadcast_to(number, (CAP, LANES))

        def add_rows(base, count):
            depth = count * CAP

            def unpack(index):
                block = recv_ref[base + index].astype(F32)
                for c in range(CUTS):
                    cell_ref[c, at8(index * CAP, CAP), :] = block[c * CAP : (c + 1) * CAP]

            loop(0, count, unpack, unroll=4)
            for c in range(CUTS):
                flip_ref[c * LANES : (c + 1) * LANES, :depth] = jnp.transpose(cell_ref[c, :depth]).astype(BF16)

            def component(q):
                lane = iota((depth, LANES), 1).astype(F32)
                number = column_ref[6, :depth]
                value = column_ref[q, :depth]
                parts = [
                    jnp.where(number == lane + part * LANES, value, 0.0).astype(BF16)
                    for part in range(pieces)
                ]
                product = dot(flip_ref[:, :depth], jnp.concatenate(parts, axis=1))
                for part in range(pieces):
                    acc_ref[q * pieces + part] += product[:, part * LANES : (part + 1) * LANES]

            loop(0, 6, component, unroll=2)

        base = 0
        for part, count in enumerate(RECV_STEPS):
            first = 1 if part == 0 else 0
            list_columns(base, count)
            drain(recv_ref, base + first, count - first, recv_sem.at[part])
            add_rows(base, count)
            base += count

    pl.run_scoped(
        collect,
        pltpu.VMEM(areas_hbm.shape, BF16),
        pltpu.VMEM((3,) + rock_hbm.shape, F32),
        pltpu.VMEM((SEND_STEPS * CAP, CELLS), F32),
        pltpu.VMEM((7, DEPTH, LANES), F32),
        pltpu.VMEM((CUTS, DEPTH, LANES), F32),
        pltpu.VMEM((CELLS, DEPTH), BF16),
    )

    def solve(d_ref, g_ref, coef_ref, field_ref):
        def fill(n):
            i, b = div(n, BANDS), rem(n, BANDS)
            rock = rock_ref[i, :, at8(b * 64, 64), :]
            for q in range(3):
                where = pl.ds((q * BANDS + b) * HALVES, HALVES)
                value = acc_ref[where, at8(i * 64, 64), :] + rock
                acc_ref[where, at8(i * 64, 64), :] = value
                if q == 1:
                    yy_ref[i, :, at8(8 + b * 64, 64), :] = value
                if q == 2:
                    zz_ref[1 + i, :, at8(b * 64, 64), :] = value

        loop(0, nz * BANDS, fill)
        coef_copies = []
        for d in (1, -1):
            ends = [
                (yy_ref.at[:, :, lines(d, False)], yy_ref.at[:, :, lines(d, True)], (0, d)),
                (zz_ref.at[planes(d, False)], zz_ref.at[planes(d, True)], (d, 0)),
            ]
            for source, target, side in ends:
                n = len(coef_copies)
                coef_copies.append(
                    pltpu.make_async_remote_copy(
                        source,
                        target,
                        coef_send.at[n],
                        coef_recv.at[n],
                        device_id=beside(*side),
                        device_id_type=MESH,
                    )
                )
        for copy in coef_copies:
            copy.start()

        def join(i, q):
            per = BANDS * HALVES
            values = join_lanes([
                acc_ref[q * per : (q + 2) * per, pl.ds(i * 64 + l, 8, stride=8), :].reshape(16 * per, LANES)
                for l in range(8)
            ])
            for k in range(2 * per):
                b, half = (k % per) // HALVES, k % HALVES
                for m, value in enumerate(values):
                    perm_ref[q + k // per, i, b * 8 : (b + 1) * 8, lanes_of(half, m)] = value[k * 8 : (k + 1) * 8]

        loop(0, nz, lambda i: join(i, 0))
        loop(0, nz // 2, lambda i: join(i, 2))
        for copy in coef_copies:
            copy.wait()

        def clear(ref, index):
            ref[index] = jnp.zeros_like(ref[index])

        every = slice(None)
        low, high = slice(0, 8), slice(ny * 8 + 8, ny * 8 + 16)
        inside = slice(1, nz + 1)

        @pl.when(z == 0)
        def _():
            clear(zz_ref, 0)

        @pl.when(z == gz_count - 1)
        def _():
            clear(zz_ref, nz + 1)

        @pl.when(h == 0)
        def _():
            clear(yy_ref, (every, every, low))

        @pl.when(h == xy_count - 1)
        def _():
            clear(yy_ref, (every, every, high))

        def prepare(n):
            i, b = div(n, BANDS), rem(n, BANDS)
            here = at8(b * 64, 64)
            where = pl.ds(b * HALVES, HALVES)
            k = acc_ref[where, at8(i * 64, 64), :]
            first = acc_ref[where, pl.ds(i * 64, 8, stride=8), :]
            last = acc_ref[where, pl.ds(i * 64 + 7, 8, stride=8), :]
            more, less = along_x(k, first, last)
            faces = [0.5 * (k + more), 0.5 * (k + less)]
            k = yy_ref[i, :, at8(b * 64 + 8, 64), :]
            faces += [0.5 * (k + yy_ref[i, :, at8(b * 64 + 16, 64), :]), 0.5 * (k + yy_ref[i, :, here, :])]
            k = zz_ref[1 + i, :, here, :]
            faces += [0.5 * (k + zz_ref[2 + i, :, here, :]), 0.5 * (k + zz_ref[i, :, here, :])]
            inverse = 1.0 / functools.reduce(lambda left, right: left + right, faces)
            for m, face in enumerate(faces):
                coef_ref[m, i, :, here, :] = face * inverse
            for m in range(3):
                cross = acc_ref[pl.ds(((3 + m) * BANDS + b) * HALVES, HALVES), at8(i * 64, 64), :]
                coef_ref[6 + m, i, :, here, :] = cross * (0.25 * inverse)
            coef_ref[9, i, :, here, :] = source_ref[i, :, here, :] * inverse

        loop(0, nz * BANDS, prepare)

        for t, weight in enumerate(STEP_WEIGHTS * SWEEPS):

            def rows_along_x(i, b, t=t):
                start = 8 + b * 64
                rows = p_ref[t, i, :, at8(start, 64), :]
                first = p_ref[t, i, :, pl.ds(start, 8, stride=8), :]
                last = p_ref[t, i, :, pl.ds(start + 7, 8, stride=8), :]
                return along_x(rows, first, last)

            def inner(i):
                for b in range(BANDS):
                    here = slice(b * 64, b * 64 + 64)
                    more, less = rows_along_x(1 + i, b)
                    d_ref[1 + i, :, 8 + b * 64 : 72 + b * 64, :] = more - less
                    g_ref[i, :, here, :] = (
                        coef_ref[9, i, :, here, :]
                        + coef_ref[0, i, :, here, :] * more
                        + coef_ref[1, i, :, here, :] * less
                    )

            def advance(n, t=t, weight=weight):
                i, y = div(n, ny // SOME), rem(n, ny // SOME) * SOME
                here = at8(y * 8, SOME * 8)
                p = lambda dz, dy: p_ref[t, i + 1 + dz, :, at8((y + 1 + dy) * 8, SOME * 8), :]
                d = lambda dz, dy: d_ref[i + 1 + dz, :, at8((y + 1 + dy) * 8, SOME * 8), :]
                coef = lambda m: coef_ref[m, i, :, here, :]
                total = g_ref[i, :, here, :]
                total = total + coef(2) * p(0, 1) + coef(3) * p(0, -1)
                total = total + coef(4) * p(1, 0) + coef(5) * p(-1, 0)
                total = total + coef(6) * (d(0, 1) - d(0, -1)) + coef(7) * (d(1, 0) - d(-1, 0))
                total = total + coef(8) * ((p(1, 1) - p(-1, 1)) - (p(1, -1) - p(-1, -1)))
                value = (1.0 - weight) * p(0, 0) + weight * total
                if t + 1 < STEPS:
                    p_ref[t + 1, i + 1, :, at8(y * 8 + 8, SOME * 8), :] = value
                else:
                    field_ref[i, :, here, :] = value

            per = ny // SOME
            loop(0, nz, inner)
            if t:
                loop(t * 2 - 2, t * 2, lambda i: join(i, 4))
            for n, side in enumerate(sides):
                if side[0] == 0:
                    halo_copy(t, n).wait()

            @pl.when(h == 0)
            def _():
                clear(p_ref, (t, inside, every, low))

            @pl.when(h == xy_count - 1)
            def _():
                clear(p_ref, (t, inside, every, high))

            for line in (low, high):
                more, less = along_x_faces(p_ref[t, inside, :, line, :])
                d_ref[inside, :, line, :] = more - less
            loop(per, (nz - 1) * per, advance)
            if t == 1:
                loop(nz // 2, nz, lambda i: join(i, 2))
            if t == 2:
                loop(nz - 2, nz, lambda i: join(i, 4))
            for n, side in enumerate(sides):
                if side[0] != 0:
                    halo_copy(t, n).wait()

            @pl.when(h == 0)
            def _():
                clear(p_ref, (t, 0, every, low))
                clear(p_ref, (t, nz + 1, every, low))

            @pl.when(h == xy_count - 1)
            def _():
                clear(p_ref, (t, 0, every, high))
                clear(p_ref, (t, nz + 1, every, high))

            @pl.when(z == 0)
            def _():
                clear(p_ref, (t, 0))

            @pl.when(z == gz_count - 1)
            def _():
                clear(p_ref, (t, nz + 1))

            for i in (0, nz + 1):
                for b in range(BANDS):
                    more, less = rows_along_x(i, b)
                    d_ref[i, :, 8 + b * 64 : 72 + b * 64, :] = more - less
            loop(0, per, advance)
            loop((nz - 1) * per, nz * per, advance)
            if t + 1 < STEPS:
                for n in range(len(sides)):
                    halo_copy(t + 1, n).start()

        def finish(i):
            spots = [(b, half) for b in range(BANDS) for half in range(HALVES)]
            values = join_lanes([
                jnp.concatenate([field_ref[i, half, pl.ds(b * 64 + l, 8, stride=8), :] for b, half in spots], axis=0)
                for l in range(8)
            ])
            for k, (b, half) in enumerate(spots):
                for m, value in enumerate(values):
                    pressure_ref[i, b * 8 : (b + 1) * 8, lanes_of(half, m)] = value[k * 8 : (k + 1) * 8]

        loop(0, nz, finish)
        drain(send_ref, 1, TOTAL - 1, send_sem)
        drain(near_out, 1, GROUPS - 1, near_send)
        drain(far_out, 1, OTHERS - 1, far_send)

    pl.run_scoped(
        solve,
        pltpu.VMEM(p_ref.shape[1:], F32),
        pltpu.VMEM(rock_ref.shape, F32),
        pltpu.VMEM((10,) + rock_ref.shape, F32),
        pltpu.VMEM(rock_ref.shape, F32),
    )


def export_kernel(perm_ref, pressure_ref, perm_out, pressure_out, sems):
    copies = [
        pltpu.make_async_copy(perm_ref.at[q], perm_out.at[q], sems.at[q]) for q in range(6)
    ] + [pltpu.make_async_copy(pressure_ref, pressure_out, sems.at[6])]
    for copy in copies:
        copy.start()
    for copy in copies:
        copy.wait()


def body(areas, angles, transm, owner, tile, live_count, rock, source, start):
    rows = areas.shape[0]
    nz, ny, nx = rock.shape
    lines = ny * 8
    vmem = pl.BlockSpec(memory_space=pltpu.VMEM)
    anywhere = pl.BlockSpec(memory_space=pl.ANY)
    block = (TOTAL, CAP * CUTS, LANES)
    brick = (nz, HALVES, lines, LANES)
    dma = pltpu.SemaphoreType.DMA
    perm, pressure = pl.pallas_call(
        kernel,
        out_shape=[
            pltpu.VMEM((6, nz, ny, nx), F32),
            pltpu.VMEM((nz, ny, nx), F32),
        ],
        in_specs=[vmem] * 8 + [pl.BlockSpec(memory_space=pltpu.HBM)] * 4,
        out_specs=[vmem, vmem],
        scratch_shapes=[
            pltpu.VMEM((8, rows), F32),
            pltpu.VMEM(block, BF16),
            pltpu.VMEM(block, BF16),
            pltpu.VMEM((GROUPS, OTHERS, 256), F32),
            pltpu.VMEM((GROUPS, OTHERS, 256), F32),
            pltpu.VMEM((OTHERS, GROUPS, 256), F32),
            pltpu.VMEM((OTHERS, GROUPS, 256), F32),
            pltpu.VMEM((256, TOTAL), F32),
            pltpu.VMEM((6 * BANDS * HALVES, CELLS, LANES), F32),
            pltpu.VMEM(brick, F32),
            pltpu.VMEM(brick, F32),
            pltpu.VMEM((STEPS, nz + 2, HALVES, lines + 16, LANES), F32),
            pltpu.VMEM((nz, HALVES, lines + 16, LANES), F32),
            pltpu.VMEM((nz + 2, HALVES, lines, LANES), F32),
            dma((4,)),
            dma,
            dma((len(RECV_STEPS),)),
            dma,
            dma,
            dma,
            dma,
            dma((STEPS, 8)),
            dma((STEPS, 8)),
            dma((4,)),
            dma((4,)),
            pltpu.SemaphoreType.REGULAR,
        ],
        compiler_params=pltpu.CompilerParams(
            collective_id=0, has_side_effects=True, vmem_limit_bytes=LIMIT << 20
        ),
    )(
        angles,
        transm.reshape(1, rows),
        owner.reshape(1, rows),
        tile.reshape(1, rows),
        live_count.reshape(1, 1),
        *permutations(),
        areas,
        rock,
        source,
        start,
    )
    return tuple(
        pl.pallas_call(
            export_kernel,
            out_shape=[jax.ShapeDtypeStruct(value.shape, F32) for value in (perm, pressure)],
            in_specs=[vmem, vmem],
            out_specs=[anywhere, anywhere],
            scratch_shapes=[dma((7,))],
            compiler_params=pltpu.CompilerParams(vmem_limit_bytes=8 << 20),
        )(perm, pressure)
    )


def solution(mesh):
    return jax.shard_map(
        body,
        mesh=mesh,
        in_specs=(
            P(("gz", "xy"), None),
            P(None, ("gz", "xy")),
            P(("gz", "xy")),
            P(("gz", "xy"), None),
            P(("gz", "xy")),
            P(("gz", "xy")),
            P("gz", "xy", None),
            P("gz", "xy", None),
            P("gz", "xy", None),
        ),
        out_specs=(P(None, "gz", "xy", None), P("gz", "xy", None)),
        check_vma=False,
    )
```

```python
import functools
import math

import jax
import jax.numpy as jnp
import numpy as np
from jax import lax
from jax.experimental import pallas as pl
from jax.experimental.pallas import tpu as pltpu
from jax.sharding import PartitionSpec as P

TILE = 8
SWEEPS = 2
CAP = 24
CELLS = TILE * TILE * TILE
LANES = 128
STEP_WEIGHTS = (
    1.0 / (1.0 - 0.7 * math.cos(math.pi / 4)),
    1.0 / (1.0 + 0.7 * math.cos(math.pi / 4)),
)
MESH = pl.DeviceIdType.MESH
F32 = jnp.float32
BF16 = jnp.bfloat16


SIZES = (4, 4, 4, 2)
TOTAL = 128
GROUPS = 8
OTHERS = 16
SEND_STEPS = 16
RECV_STEPS = (32, 32, 32, 16, 16)
DEPTH = max(RECV_STEPS) * CAP
CUTS = CELLS // LANES
HALVES = 2
BANDS = 2
SOME = 4
LIMIT = 56
STEPS = len(STEP_WEIGHTS) * SWEEPS


def rem(value, by):
    return lax.rem(value, jnp.int32(by))


def div(value, by):
    return lax.div(value, jnp.int32(by))


def place():
    gz, xy = lax.axis_index("gz"), lax.axis_index("xy")
    return gz, div(xy, 8), rem(div(xy, 2), 4), rem(xy, 2)


def offset_of(step):
    core, rest = step % 2, step // 2
    a, b, c = rest % 4, (rest // 4) % 4, rest // 16
    return a, (3 * a + b) % 4, (a + 2 * b + c) % 4, core


def partner(me, step):
    core, rest = rem(step, 2), div(step, 2)
    a, b, c = rem(rest, 4), rem(div(rest, 4), 4), div(rest, 16)
    x, y = rem(me[1] + 3 * a + b, 4), rem(me[2] + a + 2 * b + c, 4)
    return rem(me[0] + a, 4), x * 8 + y * 2 + rem(me[3] + core, 2)


def near_partner(me, u):
    return rem(me[0] + div(u, 2), 4), me[1] * 8 + me[2] * 2 + rem(me[3] + rem(u, 2), 2)


def far_partner(me, w):
    return me[0], rem(me[1] + div(w, 4), 4) * 8 + rem(me[2] + rem(w, 4), 4) * 2 + me[3]


def permutations():
    first, second, third = [np.zeros((TOTAL, TOTAL), np.float32) for _ in range(3)]
    for step in range(TOTAL):
        dz, dx, dy, dc = offset_of(step)
        u, w = dz * 2 + dc, dx * 4 + dy
        first[u * OTHERS + w, step] = 1
        second[w * GROUPS + u, u * OTHERS + w] = 1
        third[w * GROUPS + u, step] = 1
    return [jnp.asarray(m, BF16) for m in (first, second, third)]


def dot(a, b):
    return jnp.dot(a, b, preferred_element_type=F32)


def iota(shape, dim):
    return lax.broadcasted_iota(jnp.int32, shape, dim)


def loop(first, last, body, unroll=1):
    def step(n, carry):
        body(n)
        return carry

    lax.fori_loop(first, last, step, 0, unroll=unroll)


def row_slots(me, owner, live):
    rows = owner.shape[1]
    dz = ((owner >> 5) - me[0]) & 3
    dx = ((owner >> 3) - me[1]) & 3
    dy = ((owner >> 1) - me[2]) & 3
    dc = (owner - me[3]) & 1
    b = (dx - 3 * dz) & 3
    c = (dy - dz - 2 * b) & 3
    step = ((c * 4 + b) * 4 + dz) * 2 + dc
    step = jnp.where(iota((1, rows), 1) < live, step, -1)
    marks = (step == iota((TOTAL, rows), 0)).astype(F32)
    width = 256
    upper = (iota((width, width), 0) <= iota((width, width), 1)).astype(BF16)
    carry = jnp.zeros((TOTAL, 1), F32)
    ranks = []
    for block in range(rows // width):
        part = marks[:, block * width : (block + 1) * width]
        running = dot(part.astype(BF16), upper) + carry
        carry = running[:, width - 1 : width]
        ranks.append(jnp.sum(running * part, axis=0, keepdims=True) - 1.0)
    return step.astype(F32), jnp.concatenate(ranks, axis=1)


def fact_sheet(step, rank, angles, transm, tile):
    rows = step.shape[1]
    sines, cosines = jnp.sin(angles), jnp.cos(angles)
    polar_sin = sines[0:1]
    normal_x = polar_sin * cosines[1:2]
    normal_y = polar_sin * sines[1:2]
    normal_z = cosines[0:1]
    facts = [
        transm * (1.0 - normal_x * normal_x),
        transm * (1.0 - normal_y * normal_y),
        transm * (1.0 - normal_z * normal_z),
        -transm * normal_x * normal_y,
        -transm * normal_x * normal_z,
        -transm * normal_y * normal_z,
        (tile >> 8).astype(F32),
        (tile & 255).astype(F32),
    ]
    marks = (step == iota((TOTAL, rows), 0).astype(F32)).astype(F32).astype(BF16)
    chosen = (rank == iota((32, rows), 0).astype(F32)).astype(F32)
    spread = jnp.concatenate([chosen * fact for fact in facts], axis=0).astype(BF16)
    return lax.dot_general(marks, spread, (((1,), (1,)), ((), ())), preferred_element_type=F32)


def swap_groups(values):
    lane = iota(values[0].shape, 1)
    for size in (4, 2, 1):
        high = (lane // (16 * size)) % 2 == 1
        other = jnp.where(high, lane - 16 * size, lane + 16 * size)
        result = list(values)
        for i in range(8):
            if i & size == 0:
                low, up = values[i], values[i + size]
                crossed = jnp.take_along_axis(jnp.where(high, low, up), other, axis=1)
                result[i] = jnp.where(high, crossed, low)
                result[i + size] = jnp.where(high, up, crossed)
        values = result
    return values


def split_lanes(values):
    lane = iota(values[0].shape, 1)
    index = (lane % 16) * 8 + lane // 16
    return swap_groups([jnp.take_along_axis(value, index, axis=1) for value in values])


def join_lanes(values):
    lane = iota(values[0].shape, 1)
    index = (lane % 8) * 16 + lane // 8
    return [jnp.take_along_axis(value, index, axis=1) for value in swap_groups(values)]


def lanes_of(half, m):
    return slice((half * 8 + m) * LANES, (half * 8 + m + 1) * LANES)


def along_x(rows, first, last):
    shape = rows.shape
    rows = rows.reshape(shape[0], 8, 8, LANES)
    lane, l = iota(first.shape, 2), iota(rows.shape, 2)
    edge = jnp.zeros((1,) + first.shape[1:], F32)
    over = pltpu.roll(first, LANES - 1, 2)
    over = jnp.where(lane == LANES - 1, jnp.concatenate([over[1:], edge], axis=0), over)
    under = pltpu.roll(last, 1, 2)
    under = jnp.where(lane == 0, jnp.concatenate([edge, under[:-1]], axis=0), under)
    over = jnp.stack([pltpu.roll(over, 7 - k, 1) if k < 7 else over for k in range(8)], axis=1)
    under = jnp.stack([pltpu.roll(under, 8 - k, 1) if k else under for k in range(8)], axis=1)
    more = jnp.where(l == 7, over, pltpu.roll(rows, 7, 2))
    less = jnp.where(l == 0, under, pltpu.roll(rows, 1, 2))
    return more.reshape(shape), less.reshape(shape)


def along_x_faces(rows):
    lane, l = iota(rows.shape, 3), iota(rows.shape, 2)
    edge = jnp.zeros((rows.shape[0], 1) + rows.shape[2:], F32)
    up, down = pltpu.roll(rows, 7, 2), pltpu.roll(rows, 1, 2)
    over = pltpu.roll(up, LANES - 1, 3)
    over = jnp.where(lane == LANES - 1, jnp.concatenate([over[:, 1:], edge], axis=1), over)
    under = pltpu.roll(down, 1, 3)
    under = jnp.where(lane == 0, jnp.concatenate([edge, under[:, :-1]], axis=1), under)
    return jnp.where(l == 7, over, up), jnp.where(l == 0, under, down)


def at8(start, size):
    return pl.ds(start if isinstance(start, int) else pl.multiple_of(start, 8), size)


def kernel(
    angles_ref,
    transm_ref,
    owner_ref,
    tile_ref,
    live_ref,
    first_ref,
    second_ref,
    third_ref,
    areas_hbm,
    rock_hbm,
    source_hbm,
    start_hbm,
    perm_ref,
    pressure_ref,
    slot_ref,
    send_ref,
    recv_ref,
    near_out,
    near_in,
    far_out,
    far_in,
    turned_ref,
    acc_ref,
    rock_ref,
    source_ref,
    p_ref,
    yy_ref,
    zz_ref,
    load_sem,
    send_sem,
    recv_sem,
    near_send,
    near_recv,
    far_send,
    far_recv,
    halo_send,
    halo_recv,
    coef_send,
    coef_recv,
    ready_sem,
):
    me = place()
    z, h = lax.axis_index("gz"), lax.axis_index("xy")
    gz_count, xy_count = 4, 32
    nz, ny = rock_ref.shape[0], rock_ref.shape[2] // 8

    def beside(dz, dh):
        return (z + dz + gz_count) % gz_count, (h + dh + xy_count) % xy_count

    sides = [(dz, dh) for dz in (-1, 0, 1) for dh in (-1, 0, 1) if dz or dh]

    def planes(d, halo):
        if d == 0:
            return pl.ds(1, nz)
        if halo:
            return pl.ds(0, 1) if d > 0 else pl.ds(nz + 1, 1)
        return pl.ds(nz, 1) if d > 0 else pl.ds(1, 1)

    def lines(d, halo):
        if d == 0:
            return pl.ds(8, ny * 8)
        if halo:
            return pl.ds(0, 8) if d > 0 else pl.ds(ny * 8 + 8, 8)
        return pl.ds(ny * 8, 8) if d > 0 else pl.ds(8, 8)

    def halo_copy(t, n):
        dz, dh = sides[n]
        return pltpu.make_async_remote_copy(
            p_ref.at[t, planes(dz, False), :, lines(dh, False)],
            p_ref.at[t, planes(dz, True), :, lines(dh, True)],
            halo_send.at[t, n],
            halo_recv.at[t, n],
            device_id=beside(dz, dh),
            device_id_type=MESH,
        )

    def drain(ref, first, count, sem):
        part = ref.at[pl.ds(first, count)]
        pltpu.make_async_copy(part, part, sem).wait()

    def collect(areas_ref, plain_ref, picked_ref, column_ref, cell_ref, flip_ref):
        loads = [
            pltpu.make_async_copy(source, target, load_sem.at[n])
            for n, (source, target) in enumerate((
                (areas_hbm, areas_ref),
                (rock_hbm, plain_ref.at[0]),
                (source_hbm, plain_ref.at[1]),
                (start_hbm, plain_ref.at[2]),
            ))
        ]
        for load in loads:
            load.start()

        barrier = pltpu.get_barrier_semaphore()

        def greet(sem, to):
            pl.semaphore_signal(sem, inc=1, device_id=to, device_id_type=MESH)

        loop(1, GROUPS, lambda u: greet(barrier, near_partner(me, u)))
        loop(1, OTHERS, lambda w: greet(barrier, far_partner(me, w)))
        step, rank = row_slots(me, owner_ref[...], live_ref[...])
        slot_ref[0:1] = jnp.where(step >= 0, step * CAP + rank, -1.0)
        slot_ref[1:2] = step
        slot_ref[2:3] = rank
        rows = areas_ref.shape[0]

        def pick(chunk):
            base = chunk * SEND_STEPS
            wanted = (iota((SEND_STEPS * CAP, rows), 0) + base * CAP).astype(F32)
            chosen = (slot_ref[0:1] == wanted).astype(F32).astype(BF16)
            picked_ref[...] = dot(chosen, areas_ref[...])

            def pack(index):
                block = picked_ref[at8(index * CAP, CAP), :]
                parts = [block[:, c * LANES : (c + 1) * LANES] for c in range(CUTS)]
                send_ref[base + index] = jnp.concatenate(parts, axis=0).astype(BF16)

            loop(0, SEND_STEPS, pack, unroll=4)

        def send(step, part):
            pltpu.make_async_remote_copy(
                send_ref.at[step],
                recv_ref.at[step],
                send_sem,
                recv_sem.at[part],
                device_id=partner(me, step),
                device_id_type=MESH,
            ).start()

        def near_copy(u):
            pltpu.make_async_remote_copy(
                near_out.at[u],
                near_in.at[u],
                near_send,
                near_recv,
                device_id=near_partner(me, u),
                device_id_type=MESH,
            ).start()

        def far_copy(w):
            pltpu.make_async_remote_copy(
                far_out.at[w],
                far_in.at[w],
                far_send,
                far_recv,
                device_id=far_partner(me, w),
                device_id_type=MESH,
            ).start()

        sheet = fact_sheet(
            slot_ref[1:2], slot_ref[2:3], angles_ref[...], transm_ref[...], tile_ref[...]
        )
        near_out[...] = dot(first_ref[...], sheet.astype(BF16)).reshape(near_out.shape)
        pl.semaphore_wait(barrier, GROUPS + OTHERS - 2)
        loop(1, OTHERS, lambda w: greet(ready_sem, far_partner(me, w)))
        loop(1, GROUPS, near_copy)
        near_in[0] = near_out[0]
        loads[0].wait()
        pick(0)
        drain(near_in, 1, GROUPS - 1, near_recv)
        swapped = dot(second_ref[...], near_in[...].reshape(TOTAL, 256).astype(BF16))
        far_out[...] = swapped.reshape(far_out.shape)
        far_in[0] = far_out[0]
        pl.semaphore_wait(ready_sem, OTHERS - 1)
        loop(1, SEND_STEPS, lambda step: send(step, 0))
        recv_ref[0] = send_ref[0]

        def pick_and_send(chunk, part):
            pick(chunk)
            loop(0, SEND_STEPS, lambda index: send(chunk * SEND_STEPS + index, part))

        pick_and_send(1, 0)
        loop(1, OTHERS, far_copy)
        loop(2, 6, lambda chunk: pick_and_send(chunk, div(chunk, 2)))
        loop(6, 8, lambda chunk: pick_and_send(chunk, chunk - 3))

        for load in loads[1:]:
            load.wait()

        def split(i):
            for n in range(3):
                spots = [(b, half) for b in range(BANDS) for half in range(HALVES)]
                pieces = []
                for m in range(8):
                    parts = [plain_ref[n, i, b * 8 : (b + 1) * 8, lanes_of(half, m)] for b, half in spots]
                    pieces.append(jnp.concatenate(parts, axis=0))
                for l, value in enumerate(split_lanes(pieces)):
                    for k, (b, half) in enumerate(spots):
                        here = value[k * 8 : (k + 1) * 8]
                        if n == 2:
                            p_ref[0, 1 + i, half, pl.ds(8 + b * 64 + l, 8, stride=8), :] = here
                        else:
                            target = (rock_ref, source_ref)[n]
                            target[i, half, pl.ds(b * 64 + l, 8, stride=8), :] = here

        loop(0, nz, split)

        for n in range(len(sides)):
            halo_copy(0, n).start()

        drain(far_in, 1, OTHERS - 1, far_recv)
        turned_ref[...] = dot(
            jnp.transpose(far_in[...].reshape(TOTAL, 256)).astype(BF16), third_ref[...]
        )
        acc_ref[...] = jnp.zeros_like(acc_ref)
        pieces = acc_ref.shape[0] // 6

        def list_columns(base, count):
            lined = pltpu.roll(turned_ref[...], (TOTAL - base) % TOTAL, 1)
            for index in range(count):
                part = lined[:, index : index + 1]
                where = slice(index * CAP, (index + 1) * CAP)
                for v in range(6):
                    column_ref[v, where, :] = jnp.broadcast_to(part[32 * v : 32 * v + CAP], (CAP, LANES))
                number = part[192 : 192 + CAP] * 256.0 + part[224 : 224 + CAP]
                column_ref[6, where, :] = jnp.broadcast_to(number, (CAP, LANES))

        def add_rows(base, count):
            depth = count * CAP

            def unpack(index):
                block = recv_ref[base + index].astype(F32)
                for c in range(CUTS):
                    cell_ref[c, at8(index * CAP, CAP), :] = block[c * CAP : (c + 1) * CAP]

            loop(0, count, unpack, unroll=4)
            for c in range(CUTS):
                flip_ref[c * LANES : (c + 1) * LANES, :depth] = jnp.transpose(cell_ref[c, :depth]).astype(BF16)

            def component(q):
                lane = iota((depth, LANES), 1).astype(F32)
                number = column_ref[6, :depth]
                value = column_ref[q, :depth]
                parts = [
                    jnp.where(number == lane + part * LANES, value, 0.0).astype(BF16)
                    for part in range(pieces)
                ]
                product = dot(flip_ref[:, :depth], jnp.concatenate(parts, axis=1))
                for part in range(pieces):
                    acc_ref[q * pieces + part] += product[:, part * LANES : (part + 1) * LANES]

            loop(0, 6, component, unroll=2)

        base = 0
        for part, count in enumerate(RECV_STEPS):
            first = 1 if part == 0 else 0
            list_columns(base, count)
            drain(recv_ref, base + first, count - first, recv_sem.at[part])
            add_rows(base, count)
            base += count

    pl.run_scoped(
        collect,
        pltpu.VMEM(areas_hbm.shape, BF16),
        pltpu.VMEM((3,) + rock_hbm.shape, F32),
        pltpu.VMEM((SEND_STEPS * CAP, CELLS), F32),
        pltpu.VMEM((7, DEPTH, LANES), F32),
        pltpu.VMEM((CUTS, DEPTH, LANES), F32),
        pltpu.VMEM((CELLS, DEPTH), BF16),
    )

    def solve(d_ref, g_ref, coef_ref, field_ref):
        def fill(n):
            i, b = div(n, BANDS), rem(n, BANDS)
            rock = rock_ref[i, :, at8(b * 64, 64), :]
            for q in range(3):
                where = pl.ds((q * BANDS + b) * HALVES, HALVES)
                value = acc_ref[where, at8(i * 64, 64), :] + rock
                acc_ref[where, at8(i * 64, 64), :] = value
                if q == 1:
                    yy_ref[i, :, at8(8 + b * 64, 64), :] = value
                if q == 2:
                    zz_ref[1 + i, :, at8(b * 64, 64), :] = value

        loop(0, nz * BANDS, fill)
        coef_copies = []
        for d in (1, -1):
            ends = [
                (yy_ref.at[:, :, lines(d, False)], yy_ref.at[:, :, lines(d, True)], (0, d)),
                (zz_ref.at[planes(d, False)], zz_ref.at[planes(d, True)], (d, 0)),
            ]
            for source, target, side in ends:
                n = len(coef_copies)
                coef_copies.append(
                    pltpu.make_async_remote_copy(
                        source,
                        target,
                        coef_send.at[n],
                        coef_recv.at[n],
                        device_id=beside(*side),
                        device_id_type=MESH,
                    )
                )
        for copy in coef_copies:
            copy.start()

        def join(i, q):
            per = BANDS * HALVES
            values = join_lanes([
                acc_ref[q * per : (q + 2) * per, pl.ds(i * 64 + l, 8, stride=8), :].reshape(16 * per, LANES)
                for l in range(8)
            ])
            for k in range(2 * per):
                b, half = (k % per) // HALVES, k % HALVES
                for m, value in enumerate(values):
                    perm_ref[q + k // per, i, b * 8 : (b + 1) * 8, lanes_of(half, m)] = value[k * 8 : (k + 1) * 8]

        loop(0, nz, lambda i: join(i, 0))
        loop(0, nz // 2, lambda i: join(i, 2))
        for copy in coef_copies:
            copy.wait()

        def clear(ref, index):
            ref[index] = jnp.zeros_like(ref[index])

        every = slice(None)
        low, high = slice(0, 8), slice(ny * 8 + 8, ny * 8 + 16)
        inside = slice(1, nz + 1)

        @pl.when(z == 0)
        def _():
            clear(zz_ref, 0)

        @pl.when(z == gz_count - 1)
        def _():
            clear(zz_ref, nz + 1)

        @pl.when(h == 0)
        def _():
            clear(yy_ref, (every, every, low))

        @pl.when(h == xy_count - 1)
        def _():
            clear(yy_ref, (every, every, high))

        def prepare(n):
            i, b = div(n, BANDS), rem(n, BANDS)
            here = at8(b * 64, 64)
            where = pl.ds(b * HALVES, HALVES)
            k = acc_ref[where, at8(i * 64, 64), :]
            first = acc_ref[where, pl.ds(i * 64, 8, stride=8), :]
            last = acc_ref[where, pl.ds(i * 64 + 7, 8, stride=8), :]
            more, less = along_x(k, first, last)
            faces = [0.5 * (k + more), 0.5 * (k + less)]
            k = yy_ref[i, :, at8(b * 64 + 8, 64), :]
            faces += [0.5 * (k + yy_ref[i, :, at8(b * 64 + 16, 64), :]), 0.5 * (k + yy_ref[i, :, here, :])]
            k = zz_ref[1 + i, :, here, :]
            faces += [0.5 * (k + zz_ref[2 + i, :, here, :]), 0.5 * (k + zz_ref[i, :, here, :])]
            inverse = 1.0 / functools.reduce(lambda left, right: left + right, faces)
            for m, face in enumerate(faces):
                coef_ref[m, i, :, here, :] = face * inverse
            for m in range(3):
                cross = acc_ref[pl.ds(((3 + m) * BANDS + b) * HALVES, HALVES), at8(i * 64, 64), :]
                coef_ref[6 + m, i, :, here, :] = cross * (0.25 * inverse)
            coef_ref[9, i, :, here, :] = source_ref[i, :, here, :] * inverse

        loop(0, nz * BANDS, prepare)

        for t, weight in enumerate(STEP_WEIGHTS * SWEEPS):

            def rows_along_x(i, b, t=t):
                start = 8 + b * 64
                rows = p_ref[t, i, :, at8(start, 64), :]
                first = p_ref[t, i, :, pl.ds(start, 8, stride=8), :]
                last = p_ref[t, i, :, pl.ds(start + 7, 8, stride=8), :]
                return along_x(rows, first, last)

            def inner(i):
                for b in range(BANDS):
                    here = slice(b * 64, b * 64 + 64)
                    more, less = rows_along_x(1 + i, b)
                    d_ref[1 + i, :, 8 + b * 64 : 72 + b * 64, :] = more - less
                    g_ref[i, :, here, :] = (
                        coef_ref[9, i, :, here, :]
                        + coef_ref[0, i, :, here, :] * more
                        + coef_ref[1, i, :, here, :] * less
                    )

            def advance(n, t=t, weight=weight):
                i, y = div(n, ny // SOME), rem(n, ny // SOME) * SOME
                here = at8(y * 8, SOME * 8)
                p = lambda dz, dy: p_ref[t, i + 1 + dz, :, at8((y + 1 + dy) * 8, SOME * 8), :]
                d = lambda dz, dy: d_ref[i + 1 + dz, :, at8((y + 1 + dy) * 8, SOME * 8), :]
                coef = lambda m: coef_ref[m, i, :, here, :]
                total = g_ref[i, :, here, :]
                total = total + coef(2) * p(0, 1) + coef(3) * p(0, -1)
                total = total + coef(4) * p(1, 0) + coef(5) * p(-1, 0)
                total = total + coef(6) * (d(0, 1) - d(0, -1)) + coef(7) * (d(1, 0) - d(-1, 0))
                total = total + coef(8) * ((p(1, 1) - p(-1, 1)) - (p(1, -1) - p(-1, -1)))
                value = (1.0 - weight) * p(0, 0) + weight * total
                if t + 1 < STEPS:
                    p_ref[t + 1, i + 1, :, at8(y * 8 + 8, SOME * 8), :] = value
                else:
                    field_ref[i, :, here, :] = value

            per = ny // SOME
            loop(0, nz, inner)
            if t:
                loop(t * 2 - 2, t * 2, lambda i: join(i, 4))
            for n, side in enumerate(sides):
                if side[0] == 0:
                    halo_copy(t, n).wait()

            @pl.when(h == 0)
            def _():
                clear(p_ref, (t, inside, every, low))

            @pl.when(h == xy_count - 1)
            def _():
                clear(p_ref, (t, inside, every, high))

            for line in (low, high):
                more, less = along_x_faces(p_ref[t, inside, :, line, :])
                d_ref[inside, :, line, :] = more - less
            loop(per, (nz - 1) * per, advance)
            if t == 1:
                loop(nz // 2, nz, lambda i: join(i, 2))
            if t == 2:
                loop(nz - 2, nz, lambda i: join(i, 4))
            for n, side in enumerate(sides):
                if side[0] != 0:
                    halo_copy(t, n).wait()

            @pl.when(h == 0)
            def _():
                clear(p_ref, (t, 0, every, low))
                clear(p_ref, (t, nz + 1, every, low))

            @pl.when(h == xy_count - 1)
            def _():
                clear(p_ref, (t, 0, every, high))
                clear(p_ref, (t, nz + 1, every, high))

            @pl.when(z == 0)
            def _():
                clear(p_ref, (t, 0))

            @pl.when(z == gz_count - 1)
            def _():
                clear(p_ref, (t, nz + 1))

            for i in (0, nz + 1):
                for b in range(BANDS):
                    more, less = rows_along_x(i, b)
                    d_ref[i, :, 8 + b * 64 : 72 + b * 64, :] = more - less
            loop(0, per, advance)
            loop((nz - 1) * per, nz * per, advance)
            if t + 1 < STEPS:
                for n in range(len(sides)):
                    halo_copy(t + 1, n).start()

        def finish(i):
            spots = [(b, half) for b in range(BANDS) for half in range(HALVES)]
            values = join_lanes([
                jnp.concatenate([field_ref[i, half, pl.ds(b * 64 + l, 8, stride=8), :] for b, half in spots], axis=0)
                for l in range(8)
            ])
            for k, (b, half) in enumerate(spots):
                for m, value in enumerate(values):
                    pressure_ref[i, b * 8 : (b + 1) * 8, lanes_of(half, m)] = value[k * 8 : (k + 1) * 8]

        loop(0, nz, finish)
        drain(send_ref, 1, TOTAL - 1, send_sem)
        drain(near_out, 1, GROUPS - 1, near_send)
        drain(far_out, 1, OTHERS - 1, far_send)

    pl.run_scoped(
        solve,
        pltpu.VMEM(p_ref.shape[1:], F32),
        pltpu.VMEM(rock_ref.shape, F32),
        pltpu.VMEM((10,) + rock_ref.shape, F32),
        pltpu.VMEM(rock_ref.shape, F32),
    )


def export_kernel(perm_ref, pressure_ref, perm_out, pressure_out, sems):
    copies = [
        pltpu.make_async_copy(perm_ref.at[q], perm_out.at[q], sems.at[q]) for q in range(6)
    ] + [pltpu.make_async_copy(pressure_ref, pressure_out, sems.at[6])]
    for copy in copies:
        copy.start()
    for copy in copies:
        copy.wait()


def body(areas, angles, transm, owner, tile, live_count, rock, source, start):
    rows = areas.shape[0]
    nz, ny, nx = rock.shape
    lines = ny * 8
    vmem = pl.BlockSpec(memory_space=pltpu.VMEM)
    anywhere = pl.BlockSpec(memory_space=pl.ANY)
    block = (TOTAL, CAP * CUTS, LANES)
    brick = (nz, HALVES, lines, LANES)
    dma = pltpu.SemaphoreType.DMA
    perm, pressure = pl.pallas_call(
        kernel,
        out_shape=[
            pltpu.VMEM((6, nz, ny, nx), F32),
            pltpu.VMEM((nz, ny, nx), F32),
        ],
        in_specs=[vmem] * 8 + [pl.BlockSpec(memory_space=pltpu.HBM)] * 4,
        out_specs=[vmem, vmem],
        scratch_shapes=[
            pltpu.VMEM((8, rows), F32),
            pltpu.VMEM(block, BF16),
            pltpu.VMEM(block, BF16),
            pltpu.VMEM((GROUPS, OTHERS, 256), F32),
            pltpu.VMEM((GROUPS, OTHERS, 256), F32),
            pltpu.VMEM((OTHERS, GROUPS, 256), F32),
            pltpu.VMEM((OTHERS, GROUPS, 256), F32),
            pltpu.VMEM((256, TOTAL), F32),
            pltpu.VMEM((6 * BANDS * HALVES, CELLS, LANES), F32),
            pltpu.VMEM(brick, F32),
            pltpu.VMEM(brick, F32),
            pltpu.VMEM((STEPS, nz + 2, HALVES, lines + 16, LANES), F32),
            pltpu.VMEM((nz, HALVES, lines + 16, LANES), F32),
            pltpu.VMEM((nz + 2, HALVES, lines, LANES), F32),
            dma((4,)),
            dma,
            dma((len(RECV_STEPS),)),
            dma,
            dma,
            dma,
            dma,
            dma((STEPS, 8)),
            dma((STEPS, 8)),
            dma((4,)),
            dma((4,)),
            pltpu.SemaphoreType.REGULAR,
        ],
        compiler_params=pltpu.CompilerParams(
            collective_id=0, has_side_effects=True, vmem_limit_bytes=LIMIT << 20
        ),
    )(
        angles,
        transm.reshape(1, rows),
        owner.reshape(1, rows),
        tile.reshape(1, rows),
        live_count.reshape(1, 1),
        *permutations(),
        areas,
        rock,
        source,
        start,
    )
    return tuple(
        pl.pallas_call(
            export_kernel,
            out_shape=[jax.ShapeDtypeStruct(value.shape, F32) for value in (perm, pressure)],
            in_specs=[vmem, vmem],
            out_specs=[anywhere, anywhere],
            scratch_shapes=[dma((7,))],
            compiler_params=pltpu.CompilerParams(vmem_limit_bytes=8 << 20),
        )(perm, pressure)
    )


def solution(mesh):
    return jax.shard_map(
        body,
        mesh=mesh,
        in_specs=(
            P(("gz", "xy"), None),
            P(None, ("gz", "xy")),
            P(("gz", "xy")),
            P(("gz", "xy"), None),
            P(("gz", "xy")),
            P(("gz", "xy")),
            P("gz", "xy", None),
            P("gz", "xy", None),
            P("gz", "xy", None),
        ),
        out_specs=(P(None, "gz", "xy", None), P("gz", "xy", None)),
        check_vma=False,
    )
```

```python
import functools
import math

import jax
import jax.numpy as jnp
import numpy as np
from jax import lax
from jax.experimental import pallas as pl
from jax.experimental.pallas import tpu as pltpu
from jax.sharding import PartitionSpec as P

TILE = 8
SWEEPS = 2
CAP = 24
CELLS = TILE * TILE * TILE
LANES = 128
STEP_WEIGHTS = (
    1.0 / (1.0 - 0.7 * math.cos(math.pi / 4)),
    1.0 / (1.0 + 0.7 * math.cos(math.pi / 4)),
)
MESH = pl.DeviceIdType.MESH
F32 = jnp.float32
BF16 = jnp.bfloat16


SIZES = (4, 4, 4, 2)
TOTAL = 128
GROUPS = 8
OTHERS = 16
SEND_STEPS = 16
RECV_STEPS = (32, 32, 32, 16, 16)
DEPTH = max(RECV_STEPS) * CAP
CUTS = CELLS // LANES
HALVES = 2
BANDS = 2
SOME = 8
LIMIT = 56
STEPS = len(STEP_WEIGHTS) * SWEEPS


def rem(value, by):
    return lax.rem(value, jnp.int32(by))


def div(value, by):
    return lax.div(value, jnp.int32(by))


def place():
    gz, xy = lax.axis_index("gz"), lax.axis_index("xy")
    return gz, div(xy, 8), rem(div(xy, 2), 4), rem(xy, 2)


def offset_of(step):
    core, rest = step % 2, step // 2
    a, b, c = rest % 4, (rest // 4) % 4, rest // 16
    return a, (3 * a + b) % 4, (a + 2 * b + c) % 4, core


def partner(me, step):
    core, rest = rem(step, 2), div(step, 2)
    a, b, c = rem(rest, 4), rem(div(rest, 4), 4), div(rest, 16)
    x, y = rem(me[1] + 3 * a + b, 4), rem(me[2] + a + 2 * b + c, 4)
    return rem(me[0] + a, 4), x * 8 + y * 2 + rem(me[3] + core, 2)


def near_partner(me, u):
    return rem(me[0] + div(u, 2), 4), me[1] * 8 + me[2] * 2 + rem(me[3] + rem(u, 2), 2)


def far_partner(me, w):
    return me[0], rem(me[1] + div(w, 4), 4) * 8 + rem(me[2] + rem(w, 4), 4) * 2 + me[3]


def permutations():
    first, second, third = [np.zeros((TOTAL, TOTAL), np.float32) for _ in range(3)]
    for step in range(TOTAL):
        dz, dx, dy, dc = offset_of(step)
        u, w = dz * 2 + dc, dx * 4 + dy
        first[u * OTHERS + w, step] = 1
        second[w * GROUPS + u, u * OTHERS + w] = 1
        third[w * GROUPS + u, step] = 1
    return [jnp.asarray(m, BF16) for m in (first, second, third)]


def dot(a, b):
    return jnp.dot(a, b, preferred_element_type=F32)


def iota(shape, dim):
    return lax.broadcasted_iota(jnp.int32, shape, dim)


def loop(first, last, body, unroll=1):
    def step(n, carry):
        body(n)
        return carry

    lax.fori_loop(first, last, step, 0, unroll=unroll)


def row_slots(me, owner, live):
    rows = owner.shape[1]
    dz = ((owner >> 5) - me[0]) & 3
    dx = ((owner >> 3) - me[1]) & 3
    dy = ((owner >> 1) - me[2]) & 3
    dc = (owner - me[3]) & 1
    b = (dx - 3 * dz) & 3
    c = (dy - dz - 2 * b) & 3
    step = ((c * 4 + b) * 4 + dz) * 2 + dc
    step = jnp.where(iota((1, rows), 1) < live, step, -1)
    marks = (step == iota((TOTAL, rows), 0)).astype(F32)
    width = 256
    upper = (iota((width, width), 0) <= iota((width, width), 1)).astype(BF16)
    carry = jnp.zeros((TOTAL, 1), F32)
    ranks = []
    for block in range(rows // width):
        part = marks[:, block * width : (block + 1) * width]
        running = dot(part.astype(BF16), upper) + carry
        carry = running[:, width - 1 : width]
        ranks.append(jnp.sum(running * part, axis=0, keepdims=True) - 1.0)
    return step.astype(F32), jnp.concatenate(ranks, axis=1)


def fact_sheet(step, rank, angles, transm, tile):
    rows = step.shape[1]
    sines, cosines = jnp.sin(angles), jnp.cos(angles)
    polar_sin = sines[0:1]
    normal_x = polar_sin * cosines[1:2]
    normal_y = polar_sin * sines[1:2]
    normal_z = cosines[0:1]
    facts = [
        transm * (1.0 - normal_x * normal_x),
        transm * (1.0 - normal_y * normal_y),
        transm * (1.0 - normal_z * normal_z),
        -transm * normal_x * normal_y,
        -transm * normal_x * normal_z,
        -transm * normal_y * normal_z,
        (tile >> 8).astype(F32),
        (tile & 255).astype(F32),
    ]
    marks = (step == iota((TOTAL, rows), 0).astype(F32)).astype(F32).astype(BF16)
    chosen = (rank == iota((32, rows), 0).astype(F32)).astype(F32)
    spread = jnp.concatenate([chosen * fact for fact in facts], axis=0).astype(BF16)
    return lax.dot_general(marks, spread, (((1,), (1,)), ((), ())), preferred_element_type=F32)


def swap_groups(values):
    lane = iota(values[0].shape, 1)
    for size in (4, 2, 1):
        high = (lane // (16 * size)) % 2 == 1
        other = jnp.where(high, lane - 16 * size, lane + 16 * size)
        result = list(values)
        for i in range(8):
            if i & size == 0:
                low, up = values[i], values[i + size]
                crossed = jnp.take_along_axis(jnp.where(high, low, up), other, axis=1)
                result[i] = jnp.where(high, crossed, low)
                result[i + size] = jnp.where(high, up, crossed)
        values = result
    return values


def split_lanes(values):
    lane = iota(values[0].shape, 1)
    index = (lane % 16) * 8 + lane // 16
    return swap_groups([jnp.take_along_axis(value, index, axis=1) for value in values])


def join_lanes(values):
    lane = iota(values[0].shape, 1)
    index = (lane % 8) * 16 + lane // 8
    return [jnp.take_along_axis(value, index, axis=1) for value in swap_groups(values)]


def lanes_of(half, m):
    return slice((half * 8 + m) * LANES, (half * 8 + m + 1) * LANES)


def along_x(rows, first, last):
    shape = rows.shape
    rows = rows.reshape(shape[0], 8, 8, LANES)
    lane, l = iota(first.shape, 2), iota(rows.shape, 2)
    edge = jnp.zeros((1,) + first.shape[1:], F32)
    over = pltpu.roll(first, LANES - 1, 2)
    over = jnp.where(lane == LANES - 1, jnp.concatenate([over[1:], edge], axis=0), over)
    under = pltpu.roll(last, 1, 2)
    under = jnp.where(lane == 0, jnp.concatenate([edge, under[:-1]], axis=0), under)
    over = jnp.stack([pltpu.roll(over, 7 - k, 1) if k < 7 else over for k in range(8)], axis=1)
    under = jnp.stack([pltpu.roll(under, 8 - k, 1) if k else under for k in range(8)], axis=1)
    more = jnp.where(l == 7, over, pltpu.roll(rows, 7, 2))
    less = jnp.where(l == 0, under, pltpu.roll(rows, 1, 2))
    return more.reshape(shape), less.reshape(shape)


def along_x_faces(rows):
    lane, l = iota(rows.shape, 3), iota(rows.shape, 2)
    edge = jnp.zeros((rows.shape[0], 1) + rows.shape[2:], F32)
    up, down = pltpu.roll(rows, 7, 2), pltpu.roll(rows, 1, 2)
    over = pltpu.roll(up, LANES - 1, 3)
    over = jnp.where(lane == LANES - 1, jnp.concatenate([over[:, 1:], edge], axis=1), over)
    under = pltpu.roll(down, 1, 3)
    under = jnp.where(lane == 0, jnp.concatenate([edge, under[:, :-1]], axis=1), under)
    return jnp.where(l == 7, over, up), jnp.where(l == 0, under, down)


def at8(start, size):
    return pl.ds(start if isinstance(start, int) else pl.multiple_of(start, 8), size)


def kernel(
    angles_ref,
    transm_ref,
    owner_ref,
    tile_ref,
    live_ref,
    first_ref,
    second_ref,
    third_ref,
    areas_hbm,
    rock_hbm,
    source_hbm,
    start_hbm,
    perm_ref,
    pressure_ref,
    slot_ref,
    send_ref,
    recv_ref,
    near_out,
    near_in,
    far_out,
    far_in,
    turned_ref,
    acc_ref,
    rock_ref,
    source_ref,
    p_ref,
    yy_ref,
    zz_ref,
    load_sem,
    send_sem,
    recv_sem,
    near_send,
    near_recv,
    far_send,
    far_recv,
    halo_send,
    halo_recv,
    coef_send,
    coef_recv,
    ready_sem,
):
    me = place()
    z, h = lax.axis_index("gz"), lax.axis_index("xy")
    gz_count, xy_count = 4, 32
    nz, ny = rock_ref.shape[0], rock_ref.shape[2] // 8

    def beside(dz, dh):
        return (z + dz + gz_count) % gz_count, (h + dh + xy_count) % xy_count

    sides = [(-1, 0), (1, 0), (0, -1), (0, 1), (-1, -1), (-1, 1), (1, -1), (1, 1)]

    def planes(d, halo):
        if d == 0:
            return pl.ds(1, nz)
        if halo:
            return pl.ds(0, 1) if d > 0 else pl.ds(nz + 1, 1)
        return pl.ds(nz, 1) if d > 0 else pl.ds(1, 1)

    def lines(d, halo):
        if d == 0:
            return pl.ds(8, ny * 8)
        if halo:
            return pl.ds(0, 8) if d > 0 else pl.ds(ny * 8 + 8, 8)
        return pl.ds(ny * 8, 8) if d > 0 else pl.ds(8, 8)

    def halo_copy(t, n):
        dz, dh = sides[n]
        return pltpu.make_async_remote_copy(
            p_ref.at[t, planes(dz, False), :, lines(dh, False)],
            p_ref.at[t, planes(dz, True), :, lines(dh, True)],
            halo_send.at[t, n],
            halo_recv.at[t, n],
            device_id=beside(dz, dh),
            device_id_type=MESH,
        )

    def drain(ref, first, count, sem):
        part = ref.at[pl.ds(first, count)]
        pltpu.make_async_copy(part, part, sem).wait()

    def collect(areas_ref, plain_ref, picked_ref, column_ref, cell_ref, flip_ref):
        loads = [
            pltpu.make_async_copy(source, target, load_sem.at[n])
            for n, (source, target) in enumerate((
                (areas_hbm, areas_ref),
                (rock_hbm, plain_ref.at[0]),
                (source_hbm, plain_ref.at[1]),
                (start_hbm, plain_ref.at[2]),
            ))
        ]
        for load in loads:
            load.start()

        barrier = pltpu.get_barrier_semaphore()

        def greet(sem, to):
            pl.semaphore_signal(sem, inc=1, device_id=to, device_id_type=MESH)

        loop(1, GROUPS, lambda u: greet(barrier, near_partner(me, u)))
        loop(1, OTHERS, lambda w: greet(barrier, far_partner(me, w)))
        step, rank = row_slots(me, owner_ref[...], live_ref[...])
        slot_ref[0:1] = jnp.where(step >= 0, step * CAP + rank, -1.0)
        slot_ref[1:2] = step
        slot_ref[2:3] = rank
        rows = areas_ref.shape[0]

        def pick(chunk):
            base = chunk * SEND_STEPS
            wanted = (iota((SEND_STEPS * CAP, rows), 0) + base * CAP).astype(F32)
            chosen = (slot_ref[0:1] == wanted).astype(F32).astype(BF16)
            picked_ref[...] = dot(chosen, areas_ref[...])

            def pack(index):
                block = picked_ref[at8(index * CAP, CAP), :]
                parts = [block[:, c * LANES : (c + 1) * LANES] for c in range(CUTS)]
                send_ref[base + index] = jnp.concatenate(parts, axis=0).astype(BF16)

            loop(0, SEND_STEPS, pack, unroll=4)

        def send(step, part):
            pltpu.make_async_remote_copy(
                send_ref.at[step],
                recv_ref.at[step],
                send_sem,
                recv_sem.at[part],
                device_id=partner(me, step),
                device_id_type=MESH,
            ).start()

        def near_copy(u):
            pltpu.make_async_remote_copy(
                near_out.at[u],
                near_in.at[u],
                near_send,
                near_recv,
                device_id=near_partner(me, u),
                device_id_type=MESH,
            ).start()

        def far_copy(w):
            pltpu.make_async_remote_copy(
                far_out.at[w],
                far_in.at[w],
                far_send,
                far_recv,
                device_id=far_partner(me, w),
                device_id_type=MESH,
            ).start()

        sheet = fact_sheet(
            slot_ref[1:2], slot_ref[2:3], angles_ref[...], transm_ref[...], tile_ref[...]
        )
        near_out[...] = dot(first_ref[...], sheet.astype(BF16)).reshape(near_out.shape)
        pl.semaphore_wait(barrier, GROUPS + OTHERS - 2)
        loop(1, OTHERS, lambda w: greet(ready_sem, far_partner(me, w)))
        loop(1, GROUPS, near_copy)
        near_in[0] = near_out[0]
        loads[0].wait()
        pick(0)
        drain(near_in, 1, GROUPS - 1, near_recv)
        swapped = dot(second_ref[...], near_in[...].reshape(TOTAL, 256).astype(BF16))
        far_out[...] = swapped.reshape(far_out.shape)
        far_in[0] = far_out[0]
        pl.semaphore_wait(ready_sem, OTHERS - 1)
        loop(1, SEND_STEPS, lambda step: send(step, 0))
        recv_ref[0] = send_ref[0]

        def pick_and_send(chunk, part):
            pick(chunk)
            loop(0, SEND_STEPS, lambda index: send(chunk * SEND_STEPS + index, part))

        pick_and_send(1, 0)
        loop(1, OTHERS, far_copy)
        loop(2, 6, lambda chunk: pick_and_send(chunk, div(chunk, 2)))
        loop(6, 8, lambda chunk: pick_and_send(chunk, chunk - 3))

        for load in loads[1:]:
            load.wait()

        def split(i):
            for n in range(3):
                spots = [(b, half) for b in range(BANDS) for half in range(HALVES)]
                pieces = []
                for m in range(8):
                    parts = [plain_ref[n, i, b * 8 : (b + 1) * 8, lanes_of(half, m)] for b, half in spots]
                    pieces.append(jnp.concatenate(parts, axis=0))
                for l, value in enumerate(split_lanes(pieces)):
                    for k, (b, half) in enumerate(spots):
                        here = value[k * 8 : (k + 1) * 8]
                        if n == 2:
                            p_ref[0, 1 + i, half, pl.ds(8 + b * 64 + l, 8, stride=8), :] = here
                        else:
                            target = (rock_ref, source_ref)[n]
                            target[i, half, pl.ds(b * 64 + l, 8, stride=8), :] = here

        loop(0, nz, split)

        for n in range(len(sides)):
            halo_copy(0, n).start()

        drain(far_in, 1, OTHERS - 1, far_recv)
        turned_ref[...] = dot(
            jnp.transpose(far_in[...].reshape(TOTAL, 256)).astype(BF16), third_ref[...]
        )
        acc_ref[...] = jnp.zeros_like(acc_ref)
        pieces = acc_ref.shape[0] // 6

        def list_columns(base, count):
            lined = pltpu.roll(turned_ref[...], (TOTAL - base) % TOTAL, 1)
            for index in range(count):
                part = lined[:, index : index + 1]
                where = slice(index * CAP, (index + 1) * CAP)
                for v in range(6):
                    column_ref[v, where, :] = jnp.broadcast_to(part[32 * v : 32 * v + CAP], (CAP, LANES))
                number = part[192 : 192 + CAP] * 256.0 + part[224 : 224 + CAP]
                column_ref[6, where, :] = jnp.broadcast_to(number, (CAP, LANES))

        def add_rows(base, count):
            depth = count * CAP

            def unpack(index):
                block = recv_ref[base + index].astype(F32)
                for c in range(CUTS):
                    cell_ref[c, at8(index * CAP, CAP), :] = block[c * CAP : (c + 1) * CAP]

            loop(0, count, unpack, unroll=4)
            for c in range(CUTS):
                flip_ref[c * LANES : (c + 1) * LANES, :depth] = jnp.transpose(cell_ref[c, :depth]).astype(BF16)

            def component(q):
                lane = iota((depth, LANES), 1).astype(F32)
                number = column_ref[6, :depth]
                value = column_ref[q, :depth]
                parts = [
                    jnp.where(number == lane + part * LANES, value, 0.0).astype(BF16)
                    for part in range(pieces)
                ]
                product = dot(flip_ref[:, :depth], jnp.concatenate(parts, axis=1))
                for part in range(pieces):
                    acc_ref[q * pieces + part] += product[:, part * LANES : (part + 1) * LANES]

            loop(0, 6, component, unroll=2)

        base = 0
        for part, count in enumerate(RECV_STEPS):
            first = 1 if part == 0 else 0
            list_columns(base, count)
            drain(recv_ref, base + first, count - first, recv_sem.at[part])
            add_rows(base, count)
            base += count

    pl.run_scoped(
        collect,
        pltpu.VMEM(areas_hbm.shape, BF16),
        pltpu.VMEM((3,) + rock_hbm.shape, F32),
        pltpu.VMEM((SEND_STEPS * CAP, CELLS), F32),
        pltpu.VMEM((7, DEPTH, LANES), F32),
        pltpu.VMEM((CUTS, DEPTH, LANES), F32),
        pltpu.VMEM((CELLS, DEPTH), BF16),
    )

    def solve(d_ref, g_ref, coef_ref, field_ref):
        def fill(n):
            i, b = div(n, BANDS), rem(n, BANDS)
            rock = rock_ref[i, :, at8(b * 64, 64), :]
            for q in range(3):
                where = pl.ds((q * BANDS + b) * HALVES, HALVES)
                value = acc_ref[where, at8(i * 64, 64), :] + rock
                acc_ref[where, at8(i * 64, 64), :] = value
                if q == 1:
                    yy_ref[i, :, at8(8 + b * 64, 64), :] = value
                if q == 2:
                    zz_ref[1 + i, :, at8(b * 64, 64), :] = value

        loop(0, nz * BANDS, fill)
        coef_copies = []
        for d in (1, -1):
            ends = [
                (yy_ref.at[:, :, lines(d, False)], yy_ref.at[:, :, lines(d, True)], (0, d)),
                (zz_ref.at[planes(d, False)], zz_ref.at[planes(d, True)], (d, 0)),
            ]
            for source, target, side in ends:
                n = len(coef_copies)
                coef_copies.append(
                    pltpu.make_async_remote_copy(
                        source,
                        target,
                        coef_send.at[n],
                        coef_recv.at[n],
                        device_id=beside(*side),
                        device_id_type=MESH,
                    )
                )
        for copy in coef_copies:
            copy.start()

        def join(i, q):
            per = BANDS * HALVES
            values = join_lanes([
                acc_ref[q * per : (q + 2) * per, pl.ds(i * 64 + l, 8, stride=8), :].reshape(16 * per, LANES)
                for l in range(8)
            ])
            for k in range(2 * per):
                b, half = (k % per) // HALVES, k % HALVES
                for m, value in enumerate(values):
                    perm_ref[q + k // per, i, b * 8 : (b + 1) * 8, lanes_of(half, m)] = value[k * 8 : (k + 1) * 8]

        loop(0, nz, lambda i: join(i, 0))
        loop(0, nz // 2, lambda i: join(i, 2))
        for copy in coef_copies:
            copy.wait()

        def clear(ref, index):
            ref[index] = jnp.zeros_like(ref[index])

        every = slice(None)
        low, high = slice(0, 8), slice(ny * 8 + 8, ny * 8 + 16)
        inside = slice(1, nz + 1)

        @pl.when(z == 0)
        def _():
            clear(zz_ref, 0)

        @pl.when(z == gz_count - 1)
        def _():
            clear(zz_ref, nz + 1)

        @pl.when(h == 0)
        def _():
            clear(yy_ref, (every, every, low))

        @pl.when(h == xy_count - 1)
        def _():
            clear(yy_ref, (every, every, high))

        def prepare(n):
            i, b = div(n, BANDS), rem(n, BANDS)
            here = at8(b * 64, 64)
            where = pl.ds(b * HALVES, HALVES)
            k = acc_ref[where, at8(i * 64, 64), :]
            first = acc_ref[where, pl.ds(i * 64, 8, stride=8), :]
            last = acc_ref[where, pl.ds(i * 64 + 7, 8, stride=8), :]
            more, less = along_x(k, first, last)
            faces = [0.5 * (k + more), 0.5 * (k + less)]
            k = yy_ref[i, :, at8(b * 64 + 8, 64), :]
            faces += [0.5 * (k + yy_ref[i, :, at8(b * 64 + 16, 64), :]), 0.5 * (k + yy_ref[i, :, here, :])]
            k = zz_ref[1 + i, :, here, :]
            faces += [0.5 * (k + zz_ref[2 + i, :, here, :]), 0.5 * (k + zz_ref[i, :, here, :])]
            inverse = 1.0 / functools.reduce(lambda left, right: left + right, faces)
            for m, face in enumerate(faces):
                coef_ref[m, i, :, here, :] = face * inverse
            for m in range(3):
                cross = acc_ref[pl.ds(((3 + m) * BANDS + b) * HALVES, HALVES), at8(i * 64, 64), :]
                coef_ref[6 + m, i, :, here, :] = cross * (0.25 * inverse)
            coef_ref[9, i, :, here, :] = source_ref[i, :, here, :] * inverse

        loop(0, nz * BANDS, prepare)

        for t, weight in enumerate(STEP_WEIGHTS * SWEEPS):

            def rows_along_x(i, b, t=t):
                start = 8 + b * 64
                rows = p_ref[t, i, :, at8(start, 64), :]
                first = p_ref[t, i, :, pl.ds(start, 8, stride=8), :]
                last = p_ref[t, i, :, pl.ds(start + 7, 8, stride=8), :]
                return along_x(rows, first, last)

            def inner(i):
                for b in range(BANDS):
                    here = slice(b * 64, b * 64 + 64)
                    more, less = rows_along_x(1 + i, b)
                    d_ref[1 + i, :, 8 + b * 64 : 72 + b * 64, :] = more - less
                    g_ref[i, :, here, :] = (
                        coef_ref[9, i, :, here, :]
                        + coef_ref[0, i, :, here, :] * more
                        + coef_ref[1, i, :, here, :] * less
                    )

            def advance(n, t=t, weight=weight):
                i, y = div(n, ny // SOME), rem(n, ny // SOME) * SOME
                here = at8(y * 8, SOME * 8)
                p = lambda dz, dy: p_ref[t, i + 1 + dz, :, at8((y + 1 + dy) * 8, SOME * 8), :]
                d = lambda dz, dy: d_ref[i + 1 + dz, :, at8((y + 1 + dy) * 8, SOME * 8), :]
                coef = lambda m: coef_ref[m, i, :, here, :]
                total = g_ref[i, :, here, :]
                total = total + coef(2) * p(0, 1) + coef(3) * p(0, -1)
                total = total + coef(4) * p(1, 0) + coef(5) * p(-1, 0)
                total = total + coef(6) * (d(0, 1) - d(0, -1)) + coef(7) * (d(1, 0) - d(-1, 0))
                total = total + coef(8) * ((p(1, 1) - p(-1, 1)) - (p(1, -1) - p(-1, -1)))
                value = (1.0 - weight) * p(0, 0) + weight * total
                if t + 1 < STEPS:
                    p_ref[t + 1, i + 1, :, at8(y * 8 + 8, SOME * 8), :] = value
                else:
                    field_ref[i, :, here, :] = value

            per = ny // SOME
            loop(0, nz, inner)
            if t:
                loop(t * 2 - 2, t * 2, lambda i: join(i, 4))
            for n, side in enumerate(sides):
                if side[0] == 0:
                    halo_copy(t, n).wait()

            @pl.when(h == 0)
            def _():
                clear(p_ref, (t, inside, every, low))

            @pl.when(h == xy_count - 1)
            def _():
                clear(p_ref, (t, inside, every, high))

            for line in (low, high):
                more, less = along_x_faces(p_ref[t, inside, :, line, :])
                d_ref[inside, :, line, :] = more - less
            loop(per, (nz - 1) * per, advance)
            if t == 1:
                loop(nz // 2, nz, lambda i: join(i, 2))
            if t == 2:
                loop(nz - 2, nz, lambda i: join(i, 4))
            for n, side in enumerate(sides):
                if side[0] != 0:
                    halo_copy(t, n).wait()

            @pl.when(h == 0)
            def _():
                clear(p_ref, (t, 0, every, low))
                clear(p_ref, (t, nz + 1, every, low))

            @pl.when(h == xy_count - 1)
            def _():
                clear(p_ref, (t, 0, every, high))
                clear(p_ref, (t, nz + 1, every, high))

            @pl.when(z == 0)
            def _():
                clear(p_ref, (t, 0))

            @pl.when(z == gz_count - 1)
            def _():
                clear(p_ref, (t, nz + 1))

            for i in (0, nz + 1):
                for b in range(BANDS):
                    more, less = rows_along_x(i, b)
                    d_ref[i, :, 8 + b * 64 : 72 + b * 64, :] = more - less
            loop(0, per, advance)
            loop((nz - 1) * per, nz * per, advance)
            if t + 1 < STEPS:
                for n in range(len(sides)):
                    halo_copy(t + 1, n).start()

        def finish(i):
            spots = [(b, half) for b in range(BANDS) for half in range(HALVES)]
            values = join_lanes([
                jnp.concatenate([field_ref[i, half, pl.ds(b * 64 + l, 8, stride=8), :] for b, half in spots], axis=0)
                for l in range(8)
            ])
            for k, (b, half) in enumerate(spots):
                for m, value in enumerate(values):
                    pressure_ref[i, b * 8 : (b + 1) * 8, lanes_of(half, m)] = value[k * 8 : (k + 1) * 8]

        loop(0, nz, finish)
        drain(send_ref, 1, TOTAL - 1, send_sem)
        drain(near_out, 1, GROUPS - 1, near_send)
        drain(far_out, 1, OTHERS - 1, far_send)

    pl.run_scoped(
        solve,
        pltpu.VMEM(p_ref.shape[1:], F32),
        pltpu.VMEM(rock_ref.shape, F32),
        pltpu.VMEM((10,) + rock_ref.shape, F32),
        pltpu.VMEM(rock_ref.shape, F32),
    )


def export_kernel(perm_ref, pressure_ref, perm_out, pressure_out, sems):
    copies = [
        pltpu.make_async_copy(perm_ref.at[q], perm_out.at[q], sems.at[q]) for q in range(6)
    ] + [pltpu.make_async_copy(pressure_ref, pressure_out, sems.at[6])]
    for copy in copies:
        copy.start()
    for copy in copies:
        copy.wait()


def body(areas, angles, transm, owner, tile, live_count, rock, source, start):
    rows = areas.shape[0]
    nz, ny, nx = rock.shape
    lines = ny * 8
    vmem = pl.BlockSpec(memory_space=pltpu.VMEM)
    anywhere = pl.BlockSpec(memory_space=pl.ANY)
    block = (TOTAL, CAP * CUTS, LANES)
    brick = (nz, HALVES, lines, LANES)
    dma = pltpu.SemaphoreType.DMA
    perm, pressure = pl.pallas_call(
        kernel,
        out_shape=[
            pltpu.VMEM((6, nz, ny, nx), F32),
            pltpu.VMEM((nz, ny, nx), F32),
        ],
        in_specs=[vmem] * 8 + [pl.BlockSpec(memory_space=pltpu.HBM)] * 4,
        out_specs=[vmem, vmem],
        scratch_shapes=[
            pltpu.VMEM((8, rows), F32),
            pltpu.VMEM(block, BF16),
            pltpu.VMEM(block, BF16),
            pltpu.VMEM((GROUPS, OTHERS, 256), F32),
            pltpu.VMEM((GROUPS, OTHERS, 256), F32),
            pltpu.VMEM((OTHERS, GROUPS, 256), F32),
            pltpu.VMEM((OTHERS, GROUPS, 256), F32),
            pltpu.VMEM((256, TOTAL), F32),
            pltpu.VMEM((6 * BANDS * HALVES, CELLS, LANES), F32),
            pltpu.VMEM(brick, F32),
            pltpu.VMEM(brick, F32),
            pltpu.VMEM((STEPS, nz + 2, HALVES, lines + 16, LANES), F32),
            pltpu.VMEM((nz, HALVES, lines + 16, LANES), F32),
            pltpu.VMEM((nz + 2, HALVES, lines, LANES), F32),
            dma((4,)),
            dma,
            dma((len(RECV_STEPS),)),
            dma,
            dma,
            dma,
            dma,
            dma((STEPS, 8)),
            dma((STEPS, 8)),
            dma((4,)),
            dma((4,)),
            pltpu.SemaphoreType.REGULAR,
        ],
        compiler_params=pltpu.CompilerParams(
            collective_id=0, has_side_effects=True, vmem_limit_bytes=LIMIT << 20
        ),
    )(
        angles,
        transm.reshape(1, rows),
        owner.reshape(1, rows),
        tile.reshape(1, rows),
        live_count.reshape(1, 1),
        *permutations(),
        areas,
        rock,
        source,
        start,
    )
    return tuple(
        pl.pallas_call(
            export_kernel,
            out_shape=[jax.ShapeDtypeStruct(value.shape, F32) for value in (perm, pressure)],
            in_specs=[vmem, vmem],
            out_specs=[anywhere, anywhere],
            scratch_shapes=[dma((7,))],
            compiler_params=pltpu.CompilerParams(vmem_limit_bytes=8 << 20),
        )(perm, pressure)
    )


def solution(mesh):
    return jax.shard_map(
        body,
        mesh=mesh,
        in_specs=(
            P(("gz", "xy"), None),
            P(None, ("gz", "xy")),
            P(("gz", "xy")),
            P(("gz", "xy"), None),
            P(("gz", "xy")),
            P(("gz", "xy")),
            P("gz", "xy", None),
            P("gz", "xy", None),
            P("gz", "xy", None),
        ),
        out_specs=(P(None, "gz", "xy", None), P("gz", "xy", None)),
        check_vma=False,
    )
```
